512 devices in a mesh: blade: 64 (over z_lo, y, x), span: 8 (over z_hi, core).
Axes of the slice: x: 4, y: 4, z: 16 (z_hi: 4, z_lo: 4; z = z_hi * 4 + z_lo), core: 2. Of those that a mesh axis runs over, the one named last changes fastest.
Arguments:
- particles: float32 [11, 128, 256, 128], P(None, 'blade', 'span')
- filled: int32 [128, 256], P('blade', 'span'), may hold values from 2 to 96, as said below
- contact_pairs: int32 [2, 128, 256, 128], P(None, 'blade', 'span'), may hold values from 0 to 639, as said below
- contact_count: int32 [128, 256], P('blade', 'span'), may hold values from 32 to 128
- movers_out: int32 [2, 2, 64, 128], P(None, None, 'blade', 'span'), may hold values from 0 to 95, as said below
- movers_in: int32 [2, 2, 64, 128], P(None, None, 'blade', 'span'), may hold values from 0 to 127, as said below
- move_count: int32 [2, 64, 8], P(None, 'blade', 'span'), may hold values from 0 to 16, as said below
Outputs:
- advanced: float32 [11, 128, 256, 128], P(None, 'blade', 'span')
The draws below stay inside these ranges and needn't reach their ends.
Inputs may be any that keep to these rules, and one draw needn't show every extreme that they name: Live slots of a cell are its first filled ones. `contact_pairs`: every entry, counted or not, joins two live particles; direction 0 joins a slot with a higher slot of the same cell; directions never point outside the grid. The same pair may be listed more than once and then acts once per entry. `movers_out`: component 0 holds cells of the block (0 to 63), component 1 slots (below 96). Forward leavers sit in the block's last blade row, backward leavers in its first; within a device block and direction each leaver has its own cell, and each is a live slot. `movers_in`: component 0 holds cells of the block (0 to 63), component 1 slots. Arrivals from behind land in the block's first blade row, from ahead in its last; every slot is 96 or higher, and the 32 slots of one device block are all different. `move_count`: zero in the forward direction on the last blade device and in the backward direction on the first.
All inputs are finite; a program needn't handle non-finite values.
Results may differ from the reference program's by a relative error of at most 0.0001.
Values sent between devices are 32-bit elements; how exact they have to be, the bound alone decides.
No kernel may reach another device: no remote copies, remote signals or barrier semaphores. Data moves between devices by JAX's collectives and lax.ppermute only.
A program may use at most 64 MiB of HBM per device.

```python
import jax
import jax.numpy as jnp
from jax import lax

CB = 2
CS = 32
SLOTS = 128
FILL_MOST = 96
KC = 128
MIG = 16
NB = 128
NS = 256


def fill_counts(key):
    return jax.random.randint(jax.random.fold_in(key, 7), (NB, NS), 2, FILL_MOST + 1)


def draw_filled(key, part):
    return fill_counts(key).astype(jnp.int32)


def draw_particles(key, part):
    counts = fill_counts(key)
    occupancy_marks = (jnp.arange(SLOTS) < counts[..., None]).astype(jnp.float32)
    noise_seeds = jax.random.split(jax.random.fold_in(key, 3), 5)
    patch_extents = (NB, NS, SLOTS)
    bottom_boundary = jax.random.uniform(noise_seeds[0], (2,) + patch_extents, jnp.float32)
    powder_thickness = jax.random.uniform(noise_seeds[1], (1,) + patch_extents, jnp.float32, 0.0, 4.0)
    kinematic_advance = 0.5 * jax.random.normal(noise_seeds[2], (6,) + patch_extents, jnp.float32)
    grain_halfwidth = jnp.exp(jax.random.uniform(noise_seeds[3], (1,) + patch_extents, jnp.float32, jnp.log(0.12), jnp.log(0.25)))
    grain_warmth = jax.random.uniform(noise_seeds[4], (1,) + patch_extents, jnp.float32)
    grain_record = jnp.concatenate([bottom_boundary, powder_thickness, kinematic_advance, grain_halfwidth, grain_warmth], 0)
    return (grain_record * occupancy_marks[None]).astype(jnp.float32)


def draw_contact_pairs(key, part):
    counts = fill_counts(key)
    noise_seeds = jax.random.split(jax.random.fold_in(key, 5), 3)
    direction = jax.random.randint(noise_seeds[0], (NB, NS, KC), 0, 5)
    row_idx = jnp.arange(NB)[:, None, None]
    col_idx = jnp.arange(NS)[None, :, None]
    blocked = (row_idx == NB - 1) & ((direction == 1) | (direction == 3) | (direction == 4))
    blocked = blocked | (col_idx == NS - 1) & ((direction == 2) | (direction == 3))
    blocked = blocked | (col_idx == 0) & (direction == 4)
    direction = jnp.where(blocked, 0, direction)
    row_step = jnp.where((direction == 0) | (direction == 2), 0, 1)
    col_step = jnp.where((direction == 2) | (direction == 3), 1, jnp.where(direction == 4, -1, 0))
    own_fill = jnp.broadcast_to(counts[:, :, None], (NB, NS, KC))
    other_fill = counts[row_idx + row_step, col_idx + col_step]
    draw_one = jax.random.randint(noise_seeds[1], (NB, NS, KC), 0, 1 << 20)
    draw_two = jax.random.randint(noise_seeds[2], (NB, NS, KC), 0, 1 << 20)
    self_first = draw_one % (own_fill - 1)
    self_second = self_first + 1 + draw_two % (own_fill - 1 - self_first)
    is_self = direction == 0
    first_slot = jnp.where(is_self, self_first, draw_one % own_fill)
    second_slot = jnp.where(is_self, self_second, draw_two % other_fill)
    return jnp.stack([first_slot, direction * SLOTS + second_slot]).astype(jnp.int32)


def draw_movers_out(key, part):
    blade_blocks = NB // CB
    span_blocks = NS // CS
    counts = fill_counts(key)
    noise_seeds = jax.random.split(jax.random.fold_in(key, 9), 2)
    scores = jax.random.randint(noise_seeds[0], (2, blade_blocks, span_blocks, CS), 0, 1 << 16) * CS + jnp.arange(CS)
    columns = jnp.argsort(scores, axis=-1)[..., :MIG]
    edge_row = jnp.array([CB - 1, 0])[:, None, None, None]
    cells = edge_row * CS + columns
    global_row = jnp.arange(blade_blocks)[None, :, None, None] * CB + edge_row
    global_col = jnp.arange(span_blocks)[None, None, :, None] * CS + columns
    fill_here = counts[global_row, global_col]
    slot_ids = jax.random.randint(noise_seeds[1], (2, blade_blocks, span_blocks, MIG), 0, 1 << 20) % fill_here
    joined = jnp.stack([cells, slot_ids], 1)
    return joined.reshape(2, 2, blade_blocks, span_blocks * MIG).astype(jnp.int32)


def draw_movers_in(key, part):
    blade_blocks = NB // CB
    span_blocks = NS // CS
    spare = SLOTS - FILL_MOST
    noise_seeds = jax.random.split(jax.random.fold_in(key, 13), 2)
    columns = jax.random.randint(noise_seeds[0], (2, blade_blocks, span_blocks, MIG), 0, CS)
    edge_row = jnp.array([0, CB - 1])[:, None, None, None]
    cells = edge_row * CS + columns
    scores = jax.random.randint(noise_seeds[1], (blade_blocks, span_blocks, spare), 0, 1 << 16) * spare + jnp.arange(spare)
    chosen = jnp.argsort(scores, axis=-1)[..., :2 * MIG].reshape(blade_blocks, span_blocks, 2, MIG)
    slot_ids = FILL_MOST + jnp.transpose(chosen, (2, 0, 1, 3))
    joined = jnp.stack([cells, slot_ids], 1)
    return joined.reshape(2, 2, blade_blocks, span_blocks * MIG).astype(jnp.int32)


def draw_move_count(key, part):
    blade_blocks = NB // CB
    span_blocks = NS // CS
    counts = jax.random.randint(jax.random.fold_in(key, 17), (2, blade_blocks, span_blocks), 0, MIG + 1)
    block_idx = jnp.arange(blade_blocks)[None, :, None]
    dir_idx = jnp.arange(2)[:, None, None]
    outside = (dir_idx == 0) & (block_idx == blade_blocks - 1) | (dir_idx == 1) & (block_idx == 0)
    return jnp.where(outside, 0, counts).astype(jnp.int32)


def set_ends(values, key, low, high):
    shape = values.shape
    spot = [jax.random.randint(jax.random.fold_in(key, axis), (), 0, shape[axis]) for axis in range(len(shape))]
    values = values.at[tuple(spot)].set(low)
    longest = shape.index(max(shape))
    spot[longest] = (spot[longest] + 1) % shape[longest]
    return values.at[tuple(spot)].set(high)


def setup_inputs(seed: int = 0) -> dict:
    keys = jax.random.split(jax.random.key(seed), 8)
    return {
        "particles": draw_particles(jax.random.fold_in(keys[7], 71), 0),
        "filled": draw_filled(jax.random.fold_in(keys[7], 71), 0),
        "contact_pairs": draw_contact_pairs(jax.random.fold_in(keys[7], 71), 0),
        "contact_count": set_ends(jax.random.randint(keys[3], (NB, NS), KC // 4, KC + 1), jax.random.fold_in(keys[3], 1), KC // 4, KC).astype(jnp.int32),
        "movers_out": draw_movers_out(jax.random.fold_in(keys[7], 71), 0),
        "movers_in": draw_movers_in(jax.random.fold_in(keys[7], 71), 0),
        "move_count": draw_move_count(jax.random.fold_in(keys[7], 71), 0),
    }


spring = 4.0
normal_damp = 0.5
tangent_damp = 0.3
conduct = 40.0
timestep_length = 0.05
density = 100.0
gravity = 9.81
soft_len = 0.05

def cross_product(left_vec, right_vec):
    return jnp.stack([left_vec[1] * right_vec[2] - left_vec[2] * right_vec[1], left_vec[2] * right_vec[0] - left_vec[0] * right_vec[2], left_vec[0] * right_vec[1] - left_vec[1] * right_vec[0]])

def pair_terms(first_state, second, row_shift, col_shift, occupancy_marks):
    offset = jnp.stack([row_shift, col_shift, jnp.zeros_like(row_shift)])
    gap_vec = second[0:3] + offset - first_state[0:3]
    distance = jnp.sqrt(lax.optimization_barrier(jnp.sum(gap_vec * gap_vec, axis=0)) + soft_len * soft_len)
    normal = gap_vec / distance
    rad_first = first_state[9]
    rad_second = second[9]
    intersection = rad_first + rad_second - distance
    spin_sum = rad_first * first_state[6:9] + rad_second * second[6:9]
    relative = second[3:6] - first_state[3:6] - cross_product(spin_sum, normal)
    normal_speed = lax.optimization_barrier(jnp.sum(relative * normal, axis=0))
    friction = tangent_damp * (relative - normal_speed * normal)
    contact_force = (normal_damp * normal_speed - spring * intersection) * normal + friction
    torque_dir = cross_product(normal, friction)
    denom = jnp.where(occupancy_marks > 0, rad_first + rad_second, 1.0)
    heat_flow = 2.0 * conduct * rad_first * rad_second / denom * (second[10] - first_state[10])
    on_first = jnp.concatenate([contact_force, rad_first * torque_dir, heat_flow[None]], 0) * occupancy_marks
    on_second = jnp.concatenate([-contact_force, rad_second * torque_dir, -heat_flow[None]], 0) * occupancy_marks
    return (on_first, on_second)

def accumulate(ghosted, pairs, occupancy_marks, first_row, first_col, cumulative_sums):
    components = ghosted.shape[0]
    span_all = ghosted.shape[2]
    tile_slots = ghosted.shape[3]
    flattened = ghosted.reshape(components, -1)
    row_at = (first_row + jnp.arange(pairs.shape[1], dtype=jnp.int32))[:, None, None]
    col_at = (first_col + jnp.arange(pairs.shape[2], dtype=jnp.int32))[None, :, None]
    direction = pairs[1] // tile_slots
    target = pairs[1] % tile_slots
    row_step = jnp.where((direction == 0) | (direction == 2), 0, 1).astype(jnp.int32)
    col_step = jnp.where((direction == 2) | (direction == 3), 1, jnp.where(direction == 4, -1, 0)).astype(jnp.int32)
    first_at = ((row_at * span_all + col_at) * tile_slots + pairs[0]).reshape(-1)
    second_at = (((row_at + row_step) * span_all + col_at + col_step) * tile_slots + target).reshape(-1)
    first_state = jnp.take(flattened, first_at, axis=1)
    second = jnp.take(flattened, second_at, axis=1)
    on_first, on_second = pair_terms(first_state, second, row_step.reshape(-1).astype(jnp.float32), col_step.reshape(-1).astype(jnp.float32), occupancy_marks.reshape(-1))
    return cumulative_sums.at[:, first_at].add(on_first).at[:, second_at].add(on_second)

def advance(grain_record, cumulative_sums, occupancy_marks):
    grain_halfwidth = grain_record[9]
    safe_radius = grain_halfwidth + (1.0 - occupancy_marks)
    grain_inertia = density * safe_radius ** 3
    accel_vec = cumulative_sums[0:3] / grain_inertia
    accel_vec = jnp.concatenate([accel_vec[0:2], accel_vec[2:3] - gravity], 0)
    translational_rate = grain_record[3:6] + timestep_length * accel_vec
    spin_rate = grain_record[6:9] + timestep_length * cumulative_sums[3:6] / (0.4 * grain_inertia * safe_radius * safe_radius)
    grain_location = grain_record[0:3] + timestep_length * translational_rate
    grain_warmth = grain_record[10] + timestep_length * cumulative_sums[6] / grain_inertia
    return jnp.concatenate([grain_location, translational_rate, spin_rate, grain_halfwidth[None], grain_warmth[None]], 0) * occupancy_marks

def reference(particles, filled, contact_pairs, contact_count, movers_out, movers_in, move_count):
    components = particles.shape[0]
    ghosted = jnp.pad(particles, ((0, 0), (1, 1), (1, 1), (0, 0)))
    live_pairs = (jnp.arange(KC, dtype=jnp.int32) < contact_count[..., None]).astype(jnp.float32)
    empty = jnp.zeros((7, (NB + 2) * (NS + 2) * SLOTS), jnp.float32)

    def block_step(block_index, cumulative_sums):
        first_row = (block_index * CB).astype(jnp.int32)
        pairs = lax.dynamic_slice_in_dim(contact_pairs, first_row, CB, 1)
        occupancy_marks = lax.dynamic_slice_in_dim(live_pairs, first_row, CB, 0)
        return accumulate(ghosted, pairs, occupancy_marks, first_row + 1, 1, cumulative_sums)
    cumulative_sums = lax.fori_loop(0, NB // CB, block_step, empty)
    cumulative_sums = cumulative_sums.reshape(7, NB + 2, NS + 2, SLOTS)[:, 1:-1, 1:-1]
    occupancy_marks = (jnp.arange(SLOTS, dtype=jnp.int32) < filled[..., None]).astype(jnp.float32)
    stepped = advance(particles, cumulative_sums, occupancy_marks)
    blade_blocks = NB // CB
    span_blocks = NS // CS
    flattened = stepped.reshape(components, -1)
    block_row = jnp.arange(blade_blocks, dtype=jnp.int32)[None, :, None, None]
    block_col = jnp.arange(span_blocks, dtype=jnp.int32)[None, None, :, None]

    def global_at(cells, slot_ids):
        return ((block_row * CB + cells // CS) * NS + block_col * CS + cells % CS) * SLOTS + slot_ids
    leaving = movers_out.reshape(2, 2, blade_blocks, span_blocks, MIG)
    sources = global_at(leaving[:, 0], leaving[:, 1])
    moving = (jnp.arange(MIG, dtype=jnp.int32) < move_count[..., None]).astype(jnp.float32)
    initial = jnp.take(flattened, sources.reshape(-1), axis=1).reshape(components, 2, blade_blocks, span_blocks, MIG)
    sent = initial * moving
    signs_dir = jnp.array([-1.0, 1.0], jnp.float32).reshape(2, 1, 1, 1)
    sent = sent.at[0].add(signs_dir * moving)
    flattened = flattened.at[:, sources.reshape(-1)].set((initial * (1.0 - moving)).reshape(components, -1))
    arriving = movers_in.reshape(2, 2, blade_blocks, span_blocks, MIG)
    targets = global_at(arriving[:, 0], arriving[:, 1])
    flattened = flattened.at[:, targets[0, 1:].reshape(-1)].set(sent[:, 0, :-1].reshape(components, -1))
    flattened = flattened.at[:, targets[1, :-1].reshape(-1)].set(sent[:, 1, 1:].reshape(components, -1))
    return flattened.reshape(particles.shape)
```

```python
import functools

import jax
import jax.numpy as jnp
from jax import lax
from jax.experimental import pallas as pl
from jax.experimental.pallas import tpu as pltpu
from jax.sharding import PartitionSpec as P

spring = 4.0
normal_damp = 0.5
tangent_damp = 0.3
conduct = 40.0
timestep = 0.05
density = 100.0
gravity = 9.81
soft_len = 0.05

COMPS = 11
LANES = 128
LIVE = 96
COLS = 32
SLAB = 40
EXT = 56
BASE = 8
SOURCES = 34
row_steps = (0, 1, 0, 1, 1)
col_steps = (0, 0, 1, 1, -1)


def iota(shape, dim):
    return lax.broadcasted_iota(jnp.int32, shape, dim)


def pick(values, index):
    return jnp.take_along_axis(values, index, axis=1, mode="promise_in_bounds")


def to_column(row, size):
    n = row.shape[1]
    spread = jnp.where(iota((size, n), 0) == iota((size, n), 1), row, 0)
    return jnp.sum(spread, axis=1, keepdims=True)


def cross(a, b):
    return (
        a[1] * b[2] - a[2] * b[1],
        a[2] * b[0] - a[0] * b[2],
        a[0] * b[1] - a[1] * b[0],
    )


def pair_terms(first, second, row_shift, col_shift, listed):
    gap = (second[0] + row_shift - first[0], second[1] + col_shift - first[1], second[2] - first[2])
    dist = jnp.sqrt(gap[0] * gap[0] + gap[1] * gap[1] + gap[2] * gap[2] + soft_len * soft_len)
    inverse = 1.0 / dist
    n = tuple(g * inverse for g in gap)
    r1, r2 = first[9], second[9]
    intersection = r1 + r2 - dist
    spin = tuple(r1 * first[6 + i] + r2 * second[6 + i] for i in range(3))
    turn = cross(spin, n)
    w = tuple(second[3 + i] - first[3 + i] - turn[i] for i in range(3))
    u = w[0] * n[0] + w[1] * n[1] + w[2] * n[2]
    fric = tuple(tangent_damp * (w[i] - u * n[i]) for i in range(3))
    push = normal_damp * u - spring * intersection
    force = tuple(push * n[i] + fric[i] for i in range(3))
    torque = cross(n, fric)
    denom = jnp.where(listed, r1 + r2, 1.0)
    heat = 2.0 * conduct * r1 * r2 / denom * (second[10] - first[10])
    on_first = [*force, *(r1 * t for t in torque), heat]
    on_second = [*(-f for f in force), *(r2 * t for t in torque), -heat]
    return (
        [jnp.where(listed, t, 0.0) for t in on_first],
        [jnp.where(listed, t, 0.0) for t in on_second],
    )


def stepped(state, totals, live):
    r = state[9] + jnp.where(live, 0.0, 1.0)
    mass = density * r * r * r
    per_mass = timestep / mass
    per_inertia = timestep / (0.4 * mass * r * r)
    v = [state[3] + per_mass * totals[0], state[4] + per_mass * totals[1]]
    v.append(state[5] + per_mass * totals[2] - timestep * gravity)
    spin = [state[6 + i] + per_inertia * totals[3 + i] for i in range(3)]
    x = [state[i] + timestep * v[i] for i in range(3)]
    warmth = state[10] + per_mass * totals[6]
    return [jnp.where(live, t, 0.0) for t in [*x, *v, *spin, state[9], warmth]]


def second_states(ext, row, heading, target, headings):
    out = []
    for j in range(COMPS):
        value = None
        for d in headings:
            where = BASE + col_steps[d]
            got = pick(ext[j, row + row_steps[d], where : where + SLAB, :], target)
            value = got if value is None else jnp.where(heading == d, got, value)
        out.append(value)
    return out


def shifts(heading):
    row_shift = jnp.where((heading == 0) | (heading == 2), 0.0, 1.0)
    col_shift = jnp.where(
        (heading == 2) | (heading == 3), 1.0, jnp.where(heading == 4, -1.0, 0.0)
    )
    return row_shift, col_shift


def keep(ref, base, terms):
    for j in range(7):
        ref[base + j * SLAB : base + (j + 1) * SLAB, :] = terms[j]
    ref[base + 7 * SLAB : base + 8 * SLAB, :] = jnp.zeros((SLAB, LANES), jnp.float32)


def halves(x):
    high = x.astype(jnp.bfloat16).astype(jnp.float32)
    return jnp.concatenate([high, x - high], 0).astype(jnp.bfloat16)


def one_hot(index_row):
    hot = iota((LANES, LANES), 0) == index_row
    return jnp.where(hot, 1.0, 0.0).astype(jnp.bfloat16)


def spread(left, right):
    out = lax.dot_general(
        halves(left), right, (((1,), (1,)), ((), ())), preferred_element_type=jnp.float32
    )
    rows = left.shape[0]
    return out[:rows] + out[rows:]


def add_tile(totals, row, col, tile):
    at = pl.ds(pl.multiple_of((row * SLAB + col + 1) * 8, 8), 8)
    totals[at, :] += tile


def pack_columns(west_p, east_p, west_c, east_c, count, near, far):
    odd = lax.rem(lax.axis_index("span"), 2) == 1
    lane = iota((1, LANES), 1)
    near[...] = jnp.zeros(near.shape, jnp.float32)
    far[...] = jnp.zeros(far.shape, jnp.float32)
    for r in range(2):
        for j in range(COMPS):
            sides = []
            for p, c, at, cell in ((west_p, west_c, 0, 0), (east_p, east_c, 7, COLS - 1)):
                value = p[j, r, at : at + 1, :]
                if j < 8:
                    extra = c[j // 4, r, at : at + 1, :].astype(jnp.float32)
                    if j % 4 != 3:
                        extra = pltpu.roll(extra, LIVE - 32 * (j % 4), 1)
                    value = jnp.where(lane < LIVE, value, extra)
                elif j == 8:
                    here = jnp.where(iota((1, COLS), 1) == cell, count[r : r + 1, :], 0)
                    here = jnp.sum(here, axis=1, keepdims=True).astype(jnp.float32)
                    value = jnp.where(lane < LIVE, value, here)
                sides.append(value)
            west, east = sides
            row = r * 12 + j
            near[row : row + 1, :] = jnp.where(odd, west, east)
            far[row : row + 1, :] = jnp.where(odd, east, west)


def leavers(movers, counts, direction):
    cells = lax.rem(movers[direction, 0], COLS)
    slots = movers[direction, 1]
    n = cells.shape[1]
    number = iota((SLAB, n), 1)
    here = (iota((SLAB, n), 0) - 1 == cells) & (number < counts[direction, 0, 0])
    slot = jnp.sum(jnp.where(here, slots + 1, 0), axis=1, keepdims=True)
    which = jnp.sum(jnp.where(here, number, 0), axis=1, keepdims=True)
    return slot, which


def unpacked_lists(rows):
    lane = iota(rows[0].shape, 1)
    lists = []
    for half in range(2):
        value = rows[half * 4 + 3]
        for k in range(3):
            moved = pltpu.roll(rows[half * 4 + k], 32 * k + 32, 1)
            value = jnp.where(lane // 32 == k, moved, value)
        lists.append(value.astype(jnp.int32))
    return lists


def own_rows(
    particles, pairs, count, near, far, movers, counts, ext, lists, totals, to_near, to_far, on_first, on_second
):
    odd = lax.rem(lax.axis_index("span"), 2) == 1
    zeros = jnp.zeros((8, LANES), jnp.float32)
    for r in range(2):
        for j in range(COMPS):
            ext[j, r, 0:8, :] = zeros
            ext[j, r, 40:48, :] = zeros
            ext[j, r, 48:56, :] = zeros
            ext[j, r, 9:41, :] = particles[j, r]
            at = slice(r * 12 + j, r * 12 + j + 1)
            ext[j, r, 8:9, :] = jnp.where(odd, near[at, :], far[at, :])
            ext[j, r, 41:42, :] = jnp.where(odd, far[at, :], near[at, :])
    sides = jnp.where(odd, near[...], far[...]), jnp.where(odd, far[...], near[...])
    for r in range(2):
        lists[0, r, 32:40, :] = jnp.zeros((8, LANES), jnp.int32)
        lists[1, r, 32:40, :] = jnp.zeros((8, LANES), jnp.int32)
        lists[2, r, 32:40, :] = jnp.zeros((8, LANES), jnp.int32)
        lists[0, r, 1:33, :] = pairs[0, r]
        lists[1, r, 1:33, :] = pairs[1, r]
        lists[2, r, 1:33, :] = jnp.broadcast_to(to_column(count[r : r + 1, :], COLS), (COLS, LANES))
        for side, at in zip(sides, (0, 33)):
            rows = [side[r * 12 + j : r * 12 + j + 1, :] for j in range(9)]
            first, second = unpacked_lists(rows[:8])
            lists[0, r, at : at + 1, :] = first
            lists[1, r, at : at + 1, :] = second
            lists[2, r, at : at + 1, :] = jnp.broadcast_to(rows[8][:, LIVE : LIVE + 1], (1, LANES)).astype(jnp.int32)
    totals[...] = jnp.zeros(totals.shape, jnp.float32)
    for r in range(2):
        headings = (0, 1, 2, 3, 4) if r == 0 else (0, 2)
        first_index = lists[0, r]
        heading = lists[1, r] // LANES
        target = lax.rem(lists[1, r], LANES)
        listed = iota((SLAB, LANES), 1) < lists[2, r]
        if r == 1:
            listed = listed & ((heading == 0) | (heading == 2))
        first = [pick(ext[j, r, BASE : BASE + SLAB, :], first_index) for j in range(COMPS)]
        second = second_states(ext, r, heading, target, headings)
        row_shift, col_shift = shifts(heading)
        f, s = pair_terms(first, second, row_shift, col_shift, listed)
        keep(on_first, r * 8 * SLAB, f)
        keep(on_second, r * 8 * SLAB, s)

    for r in range(2):
        headings = (0, 1, 2, 3, 4) if r == 0 else (0, 2)

        def source(c, _, r=r, headings=headings):
            f = on_first[pl.ds(r * 8 * SLAB + c, 8, stride=SLAB), :]
            s = on_second[pl.ds(r * 8 * SLAB + c, 8, stride=SLAB), :]
            first_row = lists[0, r, pl.ds(c, 1), :]
            second_row = lists[1, r, pl.ds(c, 1), :]
            heading = second_row // LANES
            target = lax.rem(second_row, LANES)
            hot = jnp.concatenate([one_hot(first_row), one_hot(target)], 1)
            blank = jnp.zeros((8, LANES), jnp.float32)
            left = jnp.concatenate(
                [jnp.concatenate([f if d == 0 else blank, jnp.where(heading == d, s, 0.0)], 1) for d in headings],
                0,
            )
            out = spread(left, hot)
            for at, d in enumerate(headings):
                add_tile(totals, r + row_steps[d], c + col_steps[d], out[at * 8 : at * 8 + 8])
            return 0

        lax.fori_loop(0, SOURCES, source, 0, unroll=2)

    turn = lax.rem(lax.axis_index("blade"), 2)
    lane = iota((SLAB, LANES), 1)
    for out, row in ((to_near, 1 - turn), (to_far, turn)):
        slots0, which0 = leavers(movers, counts, 1)
        slots1, which1 = leavers(movers, counts, 0)
        slot = jnp.where(row == 1, slots1, slots0)
        which = jnp.where(row == 1, which1, which0)
        at_slot = jnp.broadcast_to(jnp.maximum(slot - 1, 0), (SLAB, LANES))
        info = jnp.where(lane == LIVE + 7, slot.astype(jnp.float32), which.astype(jnp.float32))
        for j in range(7):
            part = totals[pl.ds((row * SLAB + 1) * 8 + j, SLAB - 2, stride=8), :]
            part = jnp.concatenate([part, jnp.zeros((2, LANES), jnp.float32)], 0)
            info = jnp.where(lane == LIVE + j, pick(part, at_slot), info)
        for j in range(COMPS):
            value = ext[j, row, BASE : BASE + SLAB, :]
            if j < 8:
                extra = lists[j // 4, row].astype(jnp.float32)
                if j % 4 != 3:
                    extra = pltpu.roll(extra, LIVE - 32 * (j % 4), 1)
            elif j == 8:
                extra = lists[2, row].astype(jnp.float32)
            else:
                extra = info
            out[j] = jnp.where(lane < LIVE, value, extra)


def across_rows(
    ext, lists, partial, near, far, filled, movers, counts, arrivals, out, around, totals, on_first, on_second
):
    turn = lax.rem(lax.axis_index("blade"), 2) == 1
    zeros = jnp.zeros((8, LANES), jnp.float32)
    for j in range(COMPS):
        around[0, j, 0:8, :] = zeros
        around[0, j, 48:56, :] = zeros
        around[1, j, 0:8, :] = zeros
        around[1, j, 48:56, :] = zeros
        around[0, j, 8:48, :] = jnp.where(turn, near[j], far[j])
        around[1, j, 8:48, :] = jnp.where(turn, far[j], near[j])
    totals[...] = partial[...]
    lane = iota((SLAB, LANES), 1)

    def behind(j, shift=0):
        return around[0, j, BASE + shift : BASE + shift + SLAB, :]

    def ahead(j, shift=0):
        return around[1, j, BASE + shift : BASE + shift + SLAB, :]

    first_list, second_list = unpacked_lists([behind(j) for j in range(8)])
    count_behind = behind(8)[:, LIVE : LIVE + 1].astype(jnp.int32)
    sources = (
        (behind, lambda j, k: ext[j, 0, BASE + k : BASE + k + SLAB, :], first_list, second_list, count_behind),
        (lambda j: ext[j, 1, BASE : BASE + SLAB, :], ahead, lists[0, 1], lists[1, 1], lists[2, 1]),
    )
    kept = []
    for r, (mine, others, firsts, seconds, count) in enumerate(sources):
        heading = seconds // LANES
        target = lax.rem(seconds, LANES)
        listed = (lane < count) & ((heading == 1) | (heading == 3) | (heading == 4))
        first = [pick(mine(j), firsts) for j in range(COMPS)]
        second = []
        for j in range(COMPS):
            value = pick(others(j, 0), target)
            for d in (3, 4):
                value = jnp.where(heading == d, pick(others(j, col_steps[d]), target), value)
            second.append(value)
        _, col_shift = shifts(heading)
        f, s = pair_terms(first, second, 1.0, col_shift, listed)
        keep(on_first, r * 8 * SLAB, f)
        keep(on_second, r * 8 * SLAB, s)
        kept.append((firsts, heading, target))

    spare = 16 * SLAB
    on_first[spare : spare + SLAB, :] = kept[0][1].astype(jnp.float32)
    on_first[spare + SLAB : spare + 2 * SLAB, :] = kept[0][2].astype(jnp.float32)

    def source(c, _):
        f = on_first[pl.ds(8 * SLAB + c, 8, stride=SLAB), :]
        s = on_second[pl.ds(c, 8, stride=SLAB), :]
        heading = on_first[pl.ds(spare + c, 1), :].astype(jnp.int32)
        target = on_first[pl.ds(spare + SLAB + c, 1), :].astype(jnp.int32)
        first_row = lists[0, 1, pl.ds(c, 1), :]
        hot = jnp.concatenate([one_hot(first_row), one_hot(target)], 1)
        blank = jnp.zeros((8, LANES), jnp.float32)
        left = jnp.concatenate(
            [jnp.concatenate([f, blank], 1)]
            + [jnp.concatenate([blank, jnp.where(heading == d, s, 0.0)], 1) for d in (1, 3, 4)],
            0,
        )
        got = spread(left, hot)
        add_tile(totals, 1, c, got[0:8])
        for at, d in enumerate((1, 3, 4)):
            add_tile(totals, 0, c + col_steps[d], got[8 + at * 8 : 16 + at * 8])
        return 0

    lax.fori_loop(0, SOURCES, source, 0, unroll=2)

    placed = []
    for side in range(2):
        state_of = behind if side == 0 else ahead
        info = state_of(9)
        slot = info[:, LIVE + 7 : LIVE + 8].astype(jnp.int32)
        which = info[:, LIVE + 8 : LIVE + 9].astype(jnp.int32)
        leaves = slot > 0
        at_slot = jnp.broadcast_to(jnp.maximum(slot - 1, 0), (SLAB, LANES))
        leaving_totals = []
        if side == 0:
            hit = kept[0][0] == slot - 1
            for j in range(7):
                term = jnp.where(hit, on_first[j * SLAB : (j + 1) * SLAB, :], 0.0)
                leaving_totals.append(jnp.sum(term, axis=1, keepdims=True))
        else:
            heading, target = kept[1][1], kept[1][2]
            masks = {}
            for d in (1, 3, 4):
                there = pltpu.roll(slot.astype(jnp.int32) + jnp.zeros((SLAB, LANES), jnp.int32), (-col_steps[d]) % SLAB, 0)
                masks[d] = (heading == d) & (target == there - 1)
            for j in range(7):
                term = on_second[(8 + j) * SLAB : (9 + j) * SLAB, :]
                total = jnp.where(masks[1], term, 0.0)
                total = total + pltpu.roll(jnp.where(masks[3], term, 0.0), 1, 0)
                total = total + pltpu.roll(jnp.where(masks[4], term, 0.0), SLAB - 1, 0)
                leaving_totals.append(jnp.sum(total, axis=1, keepdims=True))
        leaving_totals = [t + info[:, LIVE + j : LIVE + j + 1] for j, t in enumerate(leaving_totals)]
        state = [pick(state_of(j), at_slot) for j in range(COMPS)]
        moved = stepped(state, leaving_totals, leaves)
        moved[0] = moved[0] + (-1.0 if side == 0 else 1.0)
        cells = to_column(lax.rem(arrivals[side, 0], COLS), 16)
        slots = to_column(arrivals[side, 1], 16)
        hit = slots == iota((16, LANES), 1)
        number = jnp.sum(jnp.where(hit, iota((16, LANES), 0) + 1, 0), axis=0, keepdims=True) - 1
        cell = jnp.sum(jnp.where(hit, cells, 0), axis=0, keepdims=True)
        cell = jnp.where(number >= 0, cell, -1)
        match = (which == number) & leaves
        values = [jnp.sum(jnp.where(match, m, 0.0), axis=0, keepdims=True) for m in moved]
        placed.append((cell, values))

    column = iota((COLS, LANES), 0)
    lane = iota((COLS, LANES), 1)
    for r in range(2):
        slot, _ = leavers(movers, counts, 1 - r)
        slot = slot[1 : 1 + COLS]
        live = lane < to_column(filled[r : r + 1, :], COLS)
        state = [ext[j, r, 9:41, :] for j in range(COMPS)]
        sums = [totals[pl.ds((r * SLAB + 2) * 8 + j, COLS, stride=8), :] for j in range(7)]
        rows = stepped(state, sums, live)
        stay = lane != slot - 1
        cell, values = placed[r]
        lands = column == cell
        for j in range(COMPS):
            out[j, r] = jnp.where(lands, values[j], jnp.where(stay, rows[j], 0.0))


def swapped(block, axis, start):
    pairs = []
    for i in range(start, lax.axis_size(axis) - 1, 2):
        pairs += [(i, i + 1), (i + 1, i)]
    return lax.ppermute(block, axis, pairs)


vmem = functools.partial(pl.BlockSpec, memory_space=pltpu.VMEM)
smem = functools.partial(pl.BlockSpec, memory_space=pltpu.SMEM)
params = pltpu.CompilerParams(vmem_limit_bytes=24 * 1024 * 1024)


def shape(*dims, dtype=jnp.float32):
    return jax.ShapeDtypeStruct(dims, dtype)


def body(particles, filled, contact_pairs, contact_count, movers_out, movers_in, move_count):
    columns = pl.pallas_call(
        pack_columns,
        grid=(1,),
        in_specs=[
            pl.BlockSpec((COMPS, 2, 8, LANES), lambda i: (0, 0, 0, 0)),
            pl.BlockSpec((COMPS, 2, 8, LANES), lambda i: (0, 0, 3, 0)),
            pl.BlockSpec((2, 2, 8, LANES), lambda i: (0, 0, 0, 0)),
            pl.BlockSpec((2, 2, 8, LANES), lambda i: (0, 0, 3, 0)),
            pl.BlockSpec((2, COLS), lambda i: (0, 0)),
        ],
        out_specs=[pl.BlockSpec((24, LANES), lambda i: (0, 0))] * 2,
        out_shape=[shape(24, LANES)] * 2,
        compiler_params=params,
        name="pack_columns",
    )
    near, far = columns(particles, particles, contact_pairs, contact_pairs, contact_count)
    near = swapped(near, "span", 0)
    far = swapped(far, "span", 1)
    ext, lists, partial, to_near, to_far = pl.pallas_call(
        own_rows,
        in_specs=[vmem()] * 6 + [smem()],
        out_specs=[vmem()] * 5,
        out_shape=[
            shape(COMPS, 2, EXT, LANES),
            shape(3, 2, SLAB, LANES, dtype=jnp.int32),
            shape(2 * SLAB * 8, LANES),
            shape(COMPS, SLAB, LANES),
            shape(COMPS, SLAB, LANES),
        ],
        scratch_shapes=[pltpu.VMEM((16 * SLAB, LANES), jnp.float32)] * 2,
        compiler_params=params,
        name="own_rows",
    )(particles, contact_pairs, contact_count, near, far, movers_out, move_count)
    near = swapped(to_near, "blade", 0)
    far = swapped(to_far, "blade", 1)
    return pl.pallas_call(
        across_rows,
        in_specs=[vmem()] * 7 + [smem()] + [vmem()],
        out_specs=vmem(),
        out_shape=shape(COMPS, 2, COLS, LANES),
        scratch_shapes=[
            pltpu.VMEM((2, COMPS, EXT, LANES), jnp.float32),
            pltpu.VMEM((2 * SLAB * 8, LANES), jnp.float32),
            pltpu.VMEM((18 * SLAB, LANES), jnp.float32),
            pltpu.VMEM((16 * SLAB, LANES), jnp.float32),
        ],
        compiler_params=params,
        name="across_rows",
    )(ext, lists, partial, near, far, filled, movers_out, move_count, movers_in)


def solution(mesh):
    return jax.shard_map(
        body,
        mesh=mesh,
        in_specs=(
            P(None, "blade", "span", None),
            P("blade", "span"),
            P(None, "blade", "span", None),
            P("blade", "span"),
            P(None, None, "blade", "span"),
            P(None, None, "blade", "span"),
            P(None, "blade", "span"),
        ),
        out_specs=P(None, "blade", "span", None),
        check_vma=False,
    )
```

```python
import jax
import jax.numpy as jnp
from jax import lax
from jax.experimental import pallas as pl
from jax.experimental.pallas import tpu as pltpu
from jax.sharding import PartitionSpec as P

spring = 4.0
normal_damp = 0.5
tangent_damp = 0.3
conduct = 40.0
timestep = 0.05
density = 100.0
gravity = 9.81
soft_len = 0.05

COMPS = 11
LANES = 128
LIVE = 96
COLS = 32
SLAB = 40
EXT = 56
BASE = 8
SOURCES = 34
EDGE = COMPS * COLS
PAYLOAD = EDGE + 24
row_steps = (0, 1, 0, 1, 1)
col_steps = (0, 0, 1, 1, -1)


def iota(shape, dim):
    return lax.broadcasted_iota(jnp.int32, shape, dim)


def pick(values, index):
    return jnp.take_along_axis(values, index, axis=1, mode="promise_in_bounds")


def to_column(row, size):
    n = row.shape[1]
    spread = jnp.where(iota((size, n), 0) == iota((size, n), 1), row, 0)
    return jnp.sum(spread, axis=1, keepdims=True)


def cross(a, b):
    return (
        a[1] * b[2] - a[2] * b[1],
        a[2] * b[0] - a[0] * b[2],
        a[0] * b[1] - a[1] * b[0],
    )


def pair_terms(first, second, row_shift, col_shift, listed):
    gap = (second[0] + row_shift - first[0], second[1] + col_shift - first[1], second[2] - first[2])
    dist = jnp.sqrt(gap[0] * gap[0] + gap[1] * gap[1] + gap[2] * gap[2] + soft_len * soft_len)
    inverse = 1.0 / dist
    n = tuple(g * inverse for g in gap)
    r1, r2 = first[9], second[9]
    intersection = r1 + r2 - dist
    spin = tuple(r1 * first[6 + i] + r2 * second[6 + i] for i in range(3))
    turn = cross(spin, n)
    w = tuple(second[3 + i] - first[3 + i] - turn[i] for i in range(3))
    u = w[0] * n[0] + w[1] * n[1] + w[2] * n[2]
    fric = tuple(tangent_damp * (w[i] - u * n[i]) for i in range(3))
    push = normal_damp * u - spring * intersection
    force = tuple(push * n[i] + fric[i] for i in range(3))
    torque = cross(n, fric)
    denom = jnp.where(listed, r1 + r2, 1.0)
    heat = 2.0 * conduct * r1 * r2 / denom * (second[10] - first[10])
    on_first = [*force, *(r1 * t for t in torque), heat]
    on_second = [*(-f for f in force), *(r2 * t for t in torque), -heat]
    return (
        [jnp.where(listed, t, 0.0) for t in on_first],
        [jnp.where(listed, t, 0.0) for t in on_second],
    )


def stepped(state, totals, live):
    r = state[9] + jnp.where(live, 0.0, 1.0)
    mass = density * r * r * r
    per_mass = timestep / mass
    per_inertia = timestep / (0.4 * mass * r * r)
    v = [state[3] + per_mass * totals[0], state[4] + per_mass * totals[1]]
    v.append(state[5] + per_mass * totals[2] - timestep * gravity)
    spin = [state[6 + i] + per_inertia * totals[3 + i] for i in range(3)]
    x = [state[i] + timestep * v[i] for i in range(3)]
    warmth = state[10] + per_mass * totals[6]
    return [jnp.where(live, t, 0.0) for t in [*x, *v, *spin, state[9], warmth]]


def shifts(heading):
    row_shift = jnp.where((heading == 0) | (heading == 2), 0.0, 1.0)
    col_shift = jnp.where(
        (heading == 2) | (heading == 3), 1.0, jnp.where(heading == 4, -1.0, 0.0)
    )
    return row_shift, col_shift


def keep(ref, base, terms):
    n = terms[0].shape[0]
    for j in range(7):
        ref[base + j * n : base + (j + 1) * n, :] = terms[j]
    ref[base + 7 * n : base + 8 * n, :] = jnp.zeros((n, LANES), jnp.float32)


def halves(x):
    high = x.astype(jnp.bfloat16).astype(jnp.float32)
    return jnp.concatenate([high, x - high], 0).astype(jnp.bfloat16)


def one_hot(index_row):
    hot = iota((LANES, LANES), 0) == index_row
    return jnp.where(hot, 1.0, 0.0).astype(jnp.bfloat16)


def spread(left, first_row, second_row):
    hot = jnp.concatenate([one_hot(first_row), one_hot(second_row)], 1)
    out = lax.dot_general(
        halves(left), hot, (((1,), (1,)), ((), ())), preferred_element_type=jnp.float32
    )
    rows = left.shape[0]
    return out[:rows] + out[rows:]


def packed(j, value, lists, count, info):
    lane = iota(value.shape, 1)
    if j < 8:
        extra = lists[j // 4].astype(jnp.float32)
        if j % 4 != 3:
            extra = pltpu.roll(extra, LIVE - 32 * (j % 4), 1)
    elif j == 8:
        extra = count.astype(jnp.float32)
    elif j == 9 and info is not None:
        extra = info
    else:
        return value
    return jnp.where(lane < LIVE, value, extra)


def unpacked(rows):
    lane = iota(rows[0].shape, 1)
    lists = []
    for half in range(2):
        value = rows[half * 4 + 3]
        for k in range(3):
            moved = pltpu.roll(rows[half * 4 + k], 32 * k + 32, 1)
            value = jnp.where(lane // 32 == k, moved, value)
        lists.append(value.astype(jnp.int32))
    return lists


def lane_of(value, k):
    return value[:, LIVE + k : LIVE + k + 1]


def pack_columns(particles, pairs, count, far, near, p_west, p_east, c_west, c_east, n_all, sems):
    last = COLS - 8
    copies = [
        pltpu.make_async_copy(particles.at[:, :, 0:8, :], p_west, sems.at[0]),
        pltpu.make_async_copy(particles.at[:, :, last:COLS, :], p_east, sems.at[1]),
        pltpu.make_async_copy(pairs.at[:, :, 0:8, :], c_west, sems.at[2]),
        pltpu.make_async_copy(pairs.at[:, :, last:COLS, :], c_east, sems.at[3]),
        pltpu.make_async_copy(count, n_all, sems.at[4]),
    ]
    for copy in copies:
        copy.start()
    near[...] = jnp.zeros(near.shape, jnp.float32)
    far[...] = jnp.zeros(far.shape, jnp.float32)
    odd = lax.rem(lax.axis_index("span"), 2) == 1
    for copy in copies:
        copy.wait()
    for r in range(2):
        n_row = n_all[r : r + 1, :]
        sides = []
        for p, c, at, cell in ((p_west, c_west, 0, 0), (p_east, c_east, 7, COLS - 1)):
            n = jnp.sum(jnp.where(iota((1, COLS), 1) == cell, n_row, 0), axis=1, keepdims=True)
            lists = [c[k, r, at : at + 1, :] for k in range(2)]
            sides.append([packed(j, p[j, r, at : at + 1, :], lists, n, None) for j in range(COMPS)])
        for j in range(COMPS):
            west, east = sides[0][j], sides[1][j]
            row = r * 12 + j
            near[row : row + 1, :] = jnp.where(odd, west, east)
            far[row : row + 1, :] = jnp.where(odd, east, west)


def leavers(movers, counts, row):
    direction = 1 - row
    cells = lax.rem(movers[direction, 0], COLS)
    slots = movers[direction, 1]
    n = cells.shape[1]
    number = iota((COLS, n), 1)
    here = (iota((COLS, n), 0) == cells) & (number < counts[direction, 0, 0])
    slot = jnp.sum(jnp.where(here, slots + 1, 0), axis=1, keepdims=True)
    which = jnp.sum(jnp.where(here, number, 0), axis=1, keepdims=True)
    return slot, which


def roll_cells(value, step):
    return pltpu.roll(value, step % value.shape[0], 0)


def inner_terms(
    particles, pairs, count, movers, counts, on_first, on_second, to_near, to_far, ext, infos
):
    lane = iota((COLS, LANES), 1)
    column = iota((COLS, LANES), 0)
    zeros = jnp.zeros((8, LANES), jnp.float32)
    for r in range(2):
        for j in range(COMPS):
            ext[j, r, 0:8, :] = zeros
            ext[j, r, 40:48, :] = zeros
            ext[j, r, 8:40, :] = particles[j, r]
    counted = [to_column(count[r : r + 1, :], COLS) for r in range(2)]
    hits = []
    for r in range(2):
        headings = (0, 1, 2, 3, 4) if r == 0 else (0, 2)
        first_index = pairs[0, r]
        heading = pairs[1, r] // LANES
        target = lax.rem(pairs[1, r], LANES)
        outside = (column == COLS - 1) & ((heading == 2) | (heading == 3)) | (column == 0) & (heading == 4)
        listed = (lane < counted[r]) & ~outside
        if r == 1:
            listed = listed & ((heading == 0) | (heading == 2))
        first = [pick(particles[j, r], first_index) for j in range(COMPS)]
        second = []
        for j in range(COMPS):
            value = None
            for d in headings:
                at = BASE + col_steps[d]
                got = pick(ext[j, r + row_steps[d], at : at + COLS, :], target)
                value = got if value is None else jnp.where(heading == d, got, value)
            second.append(value)
        row_shift, col_shift = shifts(heading)
        f, s = pair_terms(first, second, row_shift, col_shift, listed)
        keep(on_first, r * 8 * COLS, f)
        keep(on_second, r * 8 * COLS, s)
        hits.append((first_index, heading, target))

    for r in range(2):
        slot, which = leavers(movers, counts, r)
        wide = jnp.broadcast_to(slot - 1, (COLS, LANES))
        first_index, heading, target = hits[r]
        own_first = first_index == wide
        own_second = (heading == 0) & (target == wide)
        from_left = (heading == 2) & (target == roll_cells(wide, -1))
        if r == 1:
            _, above, aim = hits[0]
            straight = (above == 1) & (aim == wide)
            slant = (above == 3) & (aim == roll_cells(wide, -1))
            back = (above == 4) & (aim == roll_cells(wide, 1))
        info = jnp.where(lane == LIVE + 7, slot.astype(jnp.float32), which.astype(jnp.float32))
        for j in range(7):
            base = (r * 8 + j) * COLS
            f = on_first[base : base + COLS, :]
            s = on_second[base : base + COLS, :]
            total = jnp.where(own_first, f, 0.0) + jnp.where(own_second, s, 0.0)
            right = jnp.where(from_left, s, 0.0)
            if r == 1:
                u = on_second[j * COLS : (j + 1) * COLS, :]
                total = total + jnp.where(straight, u, 0.0)
                right = right + jnp.where(slant, u, 0.0)
                total = total + roll_cells(jnp.where(back, u, 0.0), -1)
            total = total + roll_cells(right, 1)
            info = jnp.where(lane == LIVE + j, jnp.sum(total, axis=1, keepdims=True), info)
        infos[r] = info

    turn = lax.rem(lax.axis_index("blade"), 2)
    for out, row in ((to_near, 1 - turn), (to_far, turn)):
        n = jnp.where(row == 1, counted[1], counted[0])
        lists = [pairs[k, row] for k in range(2)]
        for j in range(COMPS):
            value = packed(j, particles[j, row], lists, jnp.broadcast_to(n, (COLS, LANES)), infos[row])
            out[j * COLS : (j + 1) * COLS, :] = value


def edge_terms(
    got_near, got_far, sent_near, sent_far, infos, near_in, far_in, to_far, to_near, edges, edge_first, edge_second
):
    to_near[0:EDGE, :] = near_in[0:EDGE, :]
    to_far[0:EDGE, :] = far_in[0:EDGE, :]
    odd = lax.rem(lax.axis_index("span"), 2) == 1
    west = jnp.where(odd, got_near[...], got_far[...])
    east = jnp.where(odd, got_far[...], got_near[...])
    west_own = jnp.where(odd, sent_near[...], sent_far[...])
    east_own = jnp.where(odd, sent_far[...], sent_near[...])
    for k, side in enumerate((west, west_own, east_own, east)):
        for r in range(2):
            edges[pl.ds(4 * r + k, 12, stride=8), :] = side[r * 12 : r * 12 + 12]
    tile = [edges[j * 8 : j * 8 + 8, :] for j in range(COMPS)]
    first_index, second_index = unpacked(tile[:8])
    heading = second_index // LANES
    target = lax.rem(second_index, LANES)
    spot = iota((8, LANES), 0)
    lane = iota((8, LANES), 1)
    even = lax.rem(spot, 2) == 0
    listed = lane < lane_of(tile[8], 0).astype(jnp.int32)
    listed = listed & (
        ((heading == 2) & even)
        | ((heading == 3) & even & (spot < 4))
        | ((heading == 4) & ~even & (spot < 4))
    )
    first = [pick(t, first_index) for t in tile]
    second = []
    for t in tile:
        beside = pick(roll_cells(t, -1), target)
        below = pick(jnp.where(even, roll_cells(t, -5), roll_cells(t, -3)), target)
        second.append(jnp.where(heading == 2, beside, below))
    row_shift, col_shift = shifts(heading)
    f, s = pair_terms(first, second, row_shift, col_shift, listed)
    keep(edge_first, 0, f)
    keep(edge_second, 0, s)

    slots = [[lane_of(infos[r, c : c + 1, :], 7).astype(jnp.int32) for c in (0, COLS - 1)] for r in range(2)]

    def at_spots(*choices):
        value = jnp.zeros((8, LANES), jnp.int32)
        for k, slot in choices:
            value = jnp.where(spot == k, slot, value)
        return value - 1

    mine = first_index == at_spots((1, slots[0][0]), (2, slots[0][1]), (6, slots[1][1]))
    beside = (heading == 2) & (target == at_spots((0, slots[0][0]), (4, slots[1][0])))
    below = (heading != 2) & (target == at_spots((0, slots[1][0]), (3, slots[1][1])))
    sums = [jnp.zeros((8, LANES), jnp.float32)] * 3
    for j in range(7):
        for k, (hit, term) in enumerate(((mine, f[j]), (beside, s[j]), (below, s[j]))):
            total = jnp.sum(jnp.where(hit, term, 0.0), axis=1, keepdims=True)
            sums[k] = jnp.where(lane == LIVE + j, total, sums[k])
    fixes = (
        (sums[0][1:2] + sums[1][0:1], sums[0][2:3]),
        (sums[1][4:5] + sums[2][0:1], sums[0][6:7] + sums[2][3:4]),
    )
    turn = lax.rem(lax.axis_index("blade"), 2)
    for out, row in ((to_near, 1 - turn), (to_far, turn)):
        low = row == 1
        for k, c in enumerate((0, COLS - 1)):
            at = 9 * COLS + c
            out[at : at + 1, :] += jnp.where(low, fixes[1][k], fixes[0][k])
        out[EDGE : EDGE + 12, :] = jnp.where(low, east[12:24], east[0:12])
        out[EDGE + 12 : EDGE + 24, :] = jnp.where(low, west[12:24], west[0:12])


def own_sums(
    particles, pairs, count, filled, movers, counts, arrivals, on_first, on_second, edges, edge_first, edge_second,
    ext_in, sums, ext, first_low, lists_low, stays, landing, by_source0, by_source1,
):
    ext[...] = ext_in[...]
    sizes = (40, 16)
    for ref, size in ((by_source0, 40), (by_source1, 16)):
        ref[0:size, :] = jnp.zeros((size, LANES), jnp.float32)
        ref[33 * size : 34 * size, :] = jnp.zeros((size, LANES), jnp.float32)
    blank = jnp.zeros((8, LANES), jnp.float32)
    for r, (ref, headings) in enumerate(((by_source0, (0, 1, 2, 3, 4)), (by_source1, (0, 2)))):

        def source(c, _, r=r, ref=ref, headings=headings):
            f = on_first[pl.ds(r * 8 * COLS + c, 8, stride=COLS), :]
            s = on_second[pl.ds(r * 8 * COLS + c, 8, stride=COLS), :]
            second_row = pairs[1, r, pl.ds(c, 1), :]
            heading = second_row // LANES
            left = jnp.concatenate(
                [jnp.concatenate([f if d == 0 else blank, jnp.where(heading == d, s, 0.0)], 1) for d in headings],
                0,
            )
            out = spread(left, pairs[0, r, pl.ds(c, 1), :], lax.rem(second_row, LANES))
            size = sizes[r]
            ref[pl.ds(pl.multiple_of((c + 1) * size, 8), size), :] = out
            return 0

        lax.fori_loop(0, COLS, source, 0, unroll=4)
    tile = [edges[j * 8 : j * 8 + 8, :] for j in range(COMPS)]
    first_index, second_index = unpacked(tile[:8])
    heading = second_index // LANES
    target = lax.rem(second_index, LANES)
    for k in (0, 1, 2, 3, 4, 6):
        f = edge_first[pl.ds(k, 8, stride=8), :]
        s = edge_second[pl.ds(k, 8, stride=8), :]
        aim = heading[k : k + 1]
        left = jnp.concatenate(
            [
                jnp.concatenate([f, blank], 1),
                jnp.concatenate([blank, jnp.where(aim == 2, s, 0.0)], 1),
                jnp.concatenate([blank, jnp.where(aim == 2, 0.0, s)], 1),
                jnp.zeros((8, 2 * LANES), jnp.float32),
            ],
            0,
        )
        out = spread(left, first_index[k : k + 1], target[k : k + 1])
        if k == 0:
            by_source0[16:24, :] = out[8:16]
            by_source0[24:32, :] = out[16:24]
        elif k == 1:
            by_source0[40:48, :] += out[0:8]
        elif k == 2:
            by_source0[32 * 40 : 32 * 40 + 8, :] += out[0:8]
        elif k == 3:
            by_source0[33 * 40 + 32 : 33 * 40 + 40, :] = out[16:24]
        elif k == 4:
            by_source1[8:16, :] = out[8:16]
        else:
            by_source1[32 * 16 : 32 * 16 + 8, :] += out[0:8]

    def column(ref, size, tile_at, shift, j):
        return ref[pl.ds((1 + shift) * size + tile_at * 8 + j, COLS, stride=size), :]

    for j in range(7):
        sums[0, j] = column(by_source0, 40, 0, 0, j) + column(by_source0, 40, 2, -1, j)
        total = column(by_source1, 16, 0, 0, j) + column(by_source1, 16, 1, -1, j)
        total = total + column(by_source0, 40, 1, 0, j) + column(by_source0, 40, 3, -1, j)
        sums[1, j] = total + column(by_source0, 40, 4, 1, j)

    for r in range(2):
        for j in range(COMPS):
            for k, at in ((3, 40), (0, 41), (1, 42), (0, 7)):
                ext[j, r, at : at + 1, :] = tile[j][4 * r + k : 4 * r + k + 1]
    rows = jnp.concatenate([pairs[0, 1], first_index[7:8], first_index[4:5], jnp.zeros((6, LANES), jnp.int32)], 0)
    seconds = jnp.concatenate([pairs[1, 1], second_index[7:8], second_index[4:5], jnp.zeros((6, LANES), jnp.int32)], 0)
    edge_count = lane_of(tile[8], 0).astype(jnp.int32)
    n = jnp.concatenate(
        [to_column(count[1:2, :], COLS), edge_count[7:8], edge_count[4:5], jnp.zeros((6, 1), jnp.int32)], 0
    )
    lists_low[0] = rows
    lists_low[1] = jnp.where(iota((SLAB, LANES), 1) < n, seconds // LANES, -1)
    lists_low[2] = lax.rem(seconds, LANES)
    for j in range(COMPS):
        first_low[j] = pick(ext[j, 1, BASE : BASE + SLAB, :], rows)
    for r in range(2):
        slot, _ = leavers(movers, counts, r)
        lane = iota((COLS, LANES), 1)
        live = lane < to_column(filled[r : r + 1, :], COLS)
        stays[r] = jnp.where(live, jnp.where(lane != slot - 1, 2, 1), 0)
        cells = to_column(lax.rem(arrivals[r, 0], COLS), 16)
        slots = to_column(arrivals[r, 1], 16)
        hit = slots == iota((16, LANES), 1)
        number = jnp.sum(jnp.where(hit, iota((16, LANES), 0) + 1, 0), axis=0, keepdims=True) - 1
        cell = jnp.sum(jnp.where(hit, cells, 0), axis=0, keepdims=True)
        landing[8 * r : 8 * r + 1, :] = number
        landing[8 * r + 1 : 8 * r + 2, :] = jnp.where(number >= 0, cell, -1)


def across_rows(
    near, far, sums, ext, first_low, lists_low, stays, landing, out, around, on_first, on_second, indices, by_source
):
    turn = lax.rem(lax.axis_index("blade"), 2) == 1
    zeros = jnp.zeros((8, LANES), jnp.float32)
    for j in range(COMPS):
        rows = slice(j * COLS, (j + 1) * COLS)
        east, west = slice(EDGE + j, EDGE + j + 1), slice(EDGE + 12 + j, EDGE + 13 + j)
        for side, (yes, no) in enumerate(((near, far), (far, near))):
            main = jnp.where(turn, yes[rows, :], no[rows, :])
            right = jnp.where(turn, yes[east, :], no[east, :])
            left = jnp.where(turn, yes[west, :], no[west, :])
            around[side, j, 40:48, :] = zeros
            around[side, j, 8:40, :] = main
            around[side, j, 40:41, :] = right
            around[side, j, 41:42, :] = left
            around[side, j, 42:43, :] = main[0:1]
            around[side, j, 7:8, :] = left
    lane = iota((SLAB, LANES), 1)

    def behind(j):
        return around[0, j, BASE : BASE + SLAB, :]

    def ahead(j):
        return around[1, j, BASE : BASE + SLAB, :]

    firsts_behind, seconds_behind = unpacked([behind(j) for j in range(8)])
    heading_behind = jnp.where(lane < lane_of(behind(8), 0).astype(jnp.int32), seconds_behind // LANES, -1)
    kept = []
    for r in range(2):
        if r == 0:
            first = [pick(behind(j), firsts_behind) for j in range(COMPS)]
            heading, target = heading_behind, lax.rem(seconds_behind, LANES)
        else:
            first = [first_low[j] for j in range(COMPS)]
            heading, target = lists_low[1], lists_low[2]
        second = []
        for j in range(COMPS):
            value = None
            for d in (1, 3, 4):
                at = BASE + col_steps[d]
                others = ext[j, 0, at : at + SLAB, :] if r == 0 else around[1, j, at : at + SLAB, :]
                got = pick(others, target)
                value = got if value is None else jnp.where(heading == d, got, value)
            second.append(value)
        listed = (heading == 1) | (heading == 3) | (heading == 4)
        _, col_shift = shifts(heading)
        f, s = pair_terms(first, second, 1.0, col_shift, listed)
        keep(on_first, r * 8 * SLAB, f)
        keep(on_second, r * 8 * SLAB, s)
        kept.append((heading, target))
    indices[0] = kept[0][0]
    indices[1] = kept[0][1]
    blank = jnp.zeros((8, LANES), jnp.float32)

    def source(c, _):
        f = on_first[pl.ds(8 * SLAB + c, 8, stride=SLAB), :]
        s = on_second[pl.ds(c, 8, stride=SLAB), :]
        heading = indices[0, pl.ds(c, 1), :]
        left = jnp.concatenate(
            [jnp.concatenate([f, blank], 1)]
            + [jnp.concatenate([blank, jnp.where(heading == d, s, 0.0)], 1) for d in (1, 3, 4)],
            0,
        )
        got = spread(left, lists_low[0, pl.ds(c, 1), :], indices[1, pl.ds(c, 1), :])
        by_source[pl.ds(pl.multiple_of((c + 1) * 32, 8), 32), :] = got
        return 0

    lax.fori_loop(0, SOURCES, source, 0, unroll=UNROLL)
    by_source[0:32, :] = by_source[34 * 32 : 35 * 32, :]

    placed = []
    for side in range(2):
        state_of = behind if side == 0 else ahead
        info = state_of(9)[:COLS]
        slot = lane_of(info, 7).astype(jnp.int32)
        which = lane_of(info, 8).astype(jnp.int32)
        leaves = slot > 0
        leaving = []
        if side == 0:
            hit = firsts_behind[:COLS] == slot - 1
            for j in range(7):
                term = jnp.where(hit, on_first[j * SLAB : j * SLAB + COLS, :], 0.0)
                leaving.append(jnp.sum(term, axis=1, keepdims=True))
        else:
            heading, target = kept[1]
            wide = jnp.broadcast_to(slot - 1, (COLS, LANES))
            wide = jnp.concatenate([wide, jnp.full((8, LANES), -1, jnp.int32)], 0)
            up = roll_cells(wide, -1)
            up = jnp.where(iota((SLAB, LANES), 0) == 33, wide[0:1], up)
            masks = {
                1: (heading == 1) & (target == wide),
                3: (heading == 3) & (target == up),
                4: (heading == 4) & (target == roll_cells(wide, 1)),
            }
            first_cell = iota((COLS, LANES), 0) == 0
            for j in range(7):
                term = on_second[(8 + j) * SLAB : (9 + j) * SLAB, :]
                total = jnp.where(masks[1], term, 0.0)[:COLS]
                slant = jnp.where(masks[3], term, 0.0)
                slant = jnp.where(first_cell, slant[33:34], roll_cells(slant, 1)[:COLS])
                total = total + slant + roll_cells(jnp.where(masks[4], term, 0.0), -1)[:COLS]
                leaving.append(jnp.sum(total, axis=1, keepdims=True))
        leaving = [t + lane_of(info, j) for j, t in enumerate(leaving)]
        at_slot = jnp.broadcast_to(jnp.maximum(slot - 1, 0), (COLS, LANES))
        state = [pick(state_of(j)[:COLS], at_slot) for j in range(COMPS)]
        moved = stepped(state, leaving, leaves)
        moved[0] = moved[0] + (-1.0 if side == 0 else 1.0)
        match = (which == landing[8 * side : 8 * side + 1, :]) & leaves
        placed.append([jnp.sum(jnp.where(match, m, 0.0), axis=0, keepdims=True) for m in moved])

    column = iota((COLS, LANES), 0)
    for r in range(2):
        totals = []
        for j in range(7):
            total = sums[r, j]
            if r == 0:
                for k, shift in ((1, 0), (2, -1), (3, 1)):
                    total = total + by_source[pl.ds((1 + shift) * 32 + k * 8 + j, COLS, stride=32), :]
            else:
                total = total + by_source[pl.ds(32 + j, COLS, stride=32), :]
            totals.append(total)
        state = [ext[j, r, BASE : BASE + COLS, :] for j in range(COMPS)]
        rows = stepped(state, totals, stays[r] > 0)
        lands = column == landing[8 * r + 1 : 8 * r + 2, :]
        for j in range(COMPS):
            out[j, r] = jnp.where(lands, placed[r][j], jnp.where(stays[r] == 1, 0.0, rows[j]))


UNROLL = 2


def swapped(block, axis, start):
    pairs = []
    for i in range(start, lax.axis_size(axis) - 1, 2):
        pairs += [(i, i + 1), (i + 1, i)]
    return lax.ppermute(block, axis, pairs)


vmem = pl.BlockSpec(memory_space=pltpu.VMEM)
smem = pl.BlockSpec(memory_space=pltpu.SMEM)
hbm = pl.BlockSpec(memory_space=pltpu.HBM)
params = pltpu.CompilerParams(vmem_limit_bytes=24 * 1024 * 1024)


def shape(*dims, dtype=jnp.float32):
    return jax.ShapeDtypeStruct(dims, dtype)


def buffer(*dims, dtype=jnp.float32):
    return pltpu.VMEM(dims, dtype)


def body(particles, filled, contact_pairs, contact_count, movers_out, movers_in, move_count):
    ints = jnp.int32
    far, near = pl.pallas_call(
        pack_columns,
        in_specs=[hbm] * 3,
        out_specs=[vmem] * 2,
        out_shape=[shape(24, LANES)] * 2,
        scratch_shapes=[
            buffer(COMPS, 2, 8, LANES),
            buffer(COMPS, 2, 8, LANES),
            buffer(2, 2, 8, LANES, dtype=ints),
            buffer(2, 2, 8, LANES, dtype=ints),
            buffer(2, COLS, dtype=ints),
            pltpu.SemaphoreType.DMA((5,)),
        ],
        compiler_params=pltpu.CompilerParams(vmem_limit_bytes=60 * 1024 * 1024),
        name="pack_columns",
    )(particles, contact_pairs, contact_count)
    got_far = swapped(far, "span", 1)
    got_near = swapped(near, "span", 0)
    on_first, on_second, to_near, to_far, ext, infos = pl.pallas_call(
        inner_terms,
        in_specs=[vmem] * 4 + [smem],
        out_specs=[vmem] * 6,
        out_shape=[
            shape(16 * COLS, LANES),
            shape(16 * COLS, LANES),
            shape(PAYLOAD, LANES),
            shape(PAYLOAD, LANES),
            shape(COMPS, 2, EXT, LANES),
            shape(2, COLS, LANES),
        ],
        compiler_params=params,
        name="inner_terms",
    )(particles, contact_pairs, contact_count, movers_out, move_count)
    to_far, to_near, edges, edge_first, edge_second = pl.pallas_call(
        edge_terms,
        in_specs=[vmem] * 7,
        out_specs=[vmem] * 5,
        out_shape=[
            shape(PAYLOAD, LANES),
            shape(PAYLOAD, LANES),
            shape(96, LANES),
            shape(64, LANES),
            shape(64, LANES),
        ],
        compiler_params=params,
        name="edge_terms",
    )(got_near, got_far, near, far, infos, to_near, to_far)
    row_far = swapped(to_far, "blade", 1)
    row_near = swapped(to_near, "blade", 0)
    sums, ext, first_low, lists_low, stays, landing = pl.pallas_call(
        own_sums,
        in_specs=[vmem] * 5 + [smem] + [vmem] * 7,
        out_specs=[vmem] * 6,
        out_shape=[
            shape(2, 7, COLS, LANES),
            shape(COMPS, 2, EXT, LANES),
            shape(COMPS, SLAB, LANES),
            shape(3, SLAB, LANES, dtype=ints),
            shape(2, COLS, LANES, dtype=ints),
            shape(16, LANES, dtype=ints),
        ],
        scratch_shapes=[buffer(34 * 40, LANES), buffer(34 * 16, LANES)],
        compiler_params=params,
        name="own_sums",
    )(
        particles, contact_pairs, contact_count, filled, movers_out, move_count, movers_in,
        on_first, on_second, edges, edge_first, edge_second, ext,
    )
    return pl.pallas_call(
        across_rows,
        in_specs=[vmem] * 8,
        out_specs=vmem,
        out_shape=shape(COMPS, 2, COLS, LANES),
        scratch_shapes=[
            buffer(2, COMPS, EXT, LANES),
            buffer(16 * SLAB, LANES),
            buffer(16 * SLAB, LANES),
            buffer(2, SLAB, LANES, dtype=ints),
            buffer(35 * 32, LANES),
        ],
        compiler_params=params,
        name="across_rows",
    )(row_near, row_far, sums, ext, first_low, lists_low, stays, landing)


def solution(mesh):
    return jax.shard_map(
        body,
        mesh=mesh,
        in_specs=(
            P(None, "blade", "span", None),
            P("blade", "span"),
            P(None, "blade", "span", None),
            P("blade", "span"),
            P(None, None, "blade", "span"),
            P(None, None, "blade", "span"),
            P(None, "blade", "span"),
        ),
        out_specs=P(None, "blade", "span", None),
        check_vma=False,
    )
```

```python
import jax
import jax.numpy as jnp
from jax import lax
from jax.experimental import pallas as pl
from jax.experimental.pallas import tpu as pltpu
from jax.sharding import PartitionSpec as P

spring = 4.0
normal_damp = 0.5
tangent_damp = 0.3
conduct = 40.0
timestep = 0.05
density = 100.0
gravity = 9.81
soft_len = 0.05

COMPS = 11
LANES = 128
LIVE = 96
COLS = 32
SLAB = 40
EXT = 56
BASE = 8
SOURCES = 34
EDGE = COMPS * COLS
PAYLOAD = EDGE + 24
row_steps = (0, 1, 0, 1, 1)
col_steps = (0, 0, 1, 1, -1)


def iota(shape, dim):
    return lax.broadcasted_iota(jnp.int32, shape, dim)


def pick(values, index):
    return jnp.take_along_axis(values, index, axis=1, mode="promise_in_bounds")


def to_column(row, size):
    n = row.shape[1]
    spread = jnp.where(iota((size, n), 0) == iota((size, n), 1), row, 0)
    return jnp.sum(spread, axis=1, keepdims=True)


def cross(a, b):
    return (
        a[1] * b[2] - a[2] * b[1],
        a[2] * b[0] - a[0] * b[2],
        a[0] * b[1] - a[1] * b[0],
    )


def pair_terms(first, second, row_shift, col_shift, listed):
    gap = (second[0] + row_shift - first[0], second[1] + col_shift - first[1], second[2] - first[2])
    dist = jnp.sqrt(gap[0] * gap[0] + gap[1] * gap[1] + gap[2] * gap[2] + soft_len * soft_len)
    inverse = 1.0 / dist
    n = tuple(g * inverse for g in gap)
    r1, r2 = first[9], second[9]
    intersection = r1 + r2 - dist
    spin = tuple(r1 * first[6 + i] + r2 * second[6 + i] for i in range(3))
    turn = cross(spin, n)
    w = tuple(second[3 + i] - first[3 + i] - turn[i] for i in range(3))
    u = w[0] * n[0] + w[1] * n[1] + w[2] * n[2]
    fric = tuple(tangent_damp * (w[i] - u * n[i]) for i in range(3))
    push = normal_damp * u - spring * intersection
    force = tuple(push * n[i] + fric[i] for i in range(3))
    torque = cross(n, fric)
    denom = jnp.where(listed, r1 + r2, 1.0)
    heat = 2.0 * conduct * r1 * r2 / denom * (second[10] - first[10])
    on_first = [*force, *(r1 * t for t in torque), heat]
    on_second = [*(-f for f in force), *(r2 * t for t in torque), -heat]
    return (
        [jnp.where(listed, t, 0.0) for t in on_first],
        [jnp.where(listed, t, 0.0) for t in on_second],
    )


def stepped(state, totals, live):
    r = state[9] + jnp.where(live, 0.0, 1.0)
    mass = density * r * r * r
    per_mass = timestep / mass
    per_inertia = timestep / (0.4 * mass * r * r)
    v = [state[3] + per_mass * totals[0], state[4] + per_mass * totals[1]]
    v.append(state[5] + per_mass * totals[2] - timestep * gravity)
    spin = [state[6 + i] + per_inertia * totals[3 + i] for i in range(3)]
    x = [state[i] + timestep * v[i] for i in range(3)]
    warmth = state[10] + per_mass * totals[6]
    return [jnp.where(live, t, 0.0) for t in [*x, *v, *spin, state[9], warmth]]


def shifts(heading):
    row_shift = jnp.where((heading == 0) | (heading == 2), 0.0, 1.0)
    col_shift = jnp.where(
        (heading == 2) | (heading == 3), 1.0, jnp.where(heading == 4, -1.0, 0.0)
    )
    return row_shift, col_shift


def keep(ref, base, terms):
    n = terms[0].shape[0]
    for j in range(7):
        ref[base + j * n : base + (j + 1) * n, :] = terms[j]
    ref[base + 7 * n : base + 8 * n, :] = jnp.zeros((n, LANES), jnp.float32)


def halves(x):
    high = x.astype(jnp.bfloat16).astype(jnp.float32)
    return jnp.concatenate([high, x - high], 0).astype(jnp.bfloat16)


def one_hot(index_row):
    hot = iota((LANES, LANES), 0) == index_row
    return jnp.where(hot, 1.0, 0.0).astype(jnp.bfloat16)


def spread(left, *index_rows):
    hot = jnp.concatenate([one_hot(row) for row in index_rows], 1)
    out = lax.dot_general(
        halves(left), hot, (((1,), (1,)), ((), ())), preferred_element_type=jnp.float32
    )
    rows = left.shape[0]
    return out[:rows] + out[rows:]


def packed(j, value, lists, count, info):
    lane = iota(value.shape, 1)
    if j < 8:
        extra = lists[j // 4].astype(jnp.float32)
        if j % 4 != 3:
            extra = pltpu.roll(extra, LIVE - 32 * (j % 4), 1)
    elif j == 8:
        extra = count.astype(jnp.float32)
    elif j == 9 and info is not None:
        extra = info
    else:
        return value
    return jnp.where(lane < LIVE, value, extra)


def unpacked(rows):
    lane = iota(rows[0].shape, 1)
    lists = []
    for half in range(2):
        value = rows[half * 4 + 3]
        for k in range(3):
            moved = pltpu.roll(rows[half * 4 + k], 32 * k + 32, 1)
            value = jnp.where(lane // 32 == k, moved, value)
        lists.append(value.astype(jnp.int32))
    return lists


def lane_of(value, k):
    return value[:, LIVE + k : LIVE + k + 1]


def pack_columns(particles, pairs, count, far, near, p_west, p_east, c_west, c_east, n_all, sems):
    last = COLS - 8
    copies = [
        pltpu.make_async_copy(particles.at[:, :, 0:8, :], p_west, sems.at[0]),
        pltpu.make_async_copy(particles.at[:, :, last:COLS, :], p_east, sems.at[1]),
        pltpu.make_async_copy(pairs.at[:, :, 0:8, :], c_west, sems.at[2]),
        pltpu.make_async_copy(pairs.at[:, :, last:COLS, :], c_east, sems.at[3]),
        pltpu.make_async_copy(count, n_all, sems.at[4]),
    ]
    for copy in copies:
        copy.start()
    near[...] = jnp.zeros(near.shape, jnp.float32)
    far[...] = jnp.zeros(far.shape, jnp.float32)
    odd = lax.rem(lax.axis_index("span"), 2) == 1
    for copy in copies:
        copy.wait()
    for r in range(2):
        n_row = n_all[r : r + 1, :]
        sides = []
        for p, c, at, cell in ((p_west, c_west, 0, 0), (p_east, c_east, 7, COLS - 1)):
            n = jnp.sum(jnp.where(iota((1, COLS), 1) == cell, n_row, 0), axis=1, keepdims=True)
            lists = [c[k, r, at : at + 1, :] for k in range(2)]
            sides.append([packed(j, p[j, r, at : at + 1, :], lists, n, None) for j in range(COMPS)])
        for j in range(COMPS):
            west, east = sides[0][j], sides[1][j]
            row = r * 12 + j
            near[row : row + 1, :] = jnp.where(odd, west, east)
            far[row : row + 1, :] = jnp.where(odd, east, west)


def leavers(movers, counts, row):
    direction = 1 - row
    cells = lax.rem(movers[direction, 0], COLS)
    slots = movers[direction, 1]
    n = cells.shape[1]
    number = iota((COLS, n), 1)
    here = (iota((COLS, n), 0) == cells) & (number < counts[direction, 0, 0])
    slot = jnp.sum(jnp.where(here, slots + 1, 0), axis=1, keepdims=True)
    which = jnp.sum(jnp.where(here, number, 0), axis=1, keepdims=True)
    return slot, which


def roll_cells(value, step):
    return pltpu.roll(value, step % value.shape[0], 0)


def inner_terms(
    particles, pairs, count, filled, movers, arrivals, counts,
    on_first, on_second, to_near, to_far, ext, infos, stays, landing,
):
    lane = iota((COLS, LANES), 1)
    column = iota((COLS, LANES), 0)
    zeros = jnp.zeros((8, LANES), jnp.float32)
    for r in range(2):
        for j in range(COMPS):
            ext[j, r, 0:8, :] = zeros
            ext[j, r, 40:48, :] = zeros
            ext[j, r, 8:40, :] = particles[j, r]
    counted = [to_column(count[r : r + 1, :], COLS) for r in range(2)]
    hits = []
    for r in range(2):
        headings = (0, 1, 2, 3, 4) if r == 0 else (0, 2)
        first_index = pairs[0, r]
        heading = pairs[1, r] // LANES
        target = lax.rem(pairs[1, r], LANES)
        outside = (column == COLS - 1) & ((heading == 2) | (heading == 3)) | (column == 0) & (heading == 4)
        listed = (lane < counted[r]) & ~outside
        if r == 1:
            listed = listed & ((heading == 0) | (heading == 2))
        first = [pick(particles[j, r], first_index) for j in range(COMPS)]
        second = []
        for j in range(COMPS):
            value = None
            for d in headings:
                at = BASE + col_steps[d]
                got = pick(ext[j, r + row_steps[d], at : at + COLS, :], target)
                value = got if value is None else jnp.where(heading == d, got, value)
            second.append(value)
        row_shift, col_shift = shifts(heading)
        f, s = pair_terms(first, second, row_shift, col_shift, listed)
        keep(on_first, r * 8 * COLS, f)
        keep(on_second, r * 8 * COLS, s)
        hits.append((first_index, heading, target))

    for r in range(2):
        slot, which = leavers(movers, counts, r)
        live = lane < to_column(filled[r : r + 1, :], COLS)
        stays[r] = jnp.where(live, jnp.where(lane != slot - 1, 2, 1), 0)
        cells = to_column(lax.rem(arrivals[r, 0], COLS), 16)
        slots = to_column(arrivals[r, 1], 16)
        hit = slots == iota((16, LANES), 1)
        number = jnp.sum(jnp.where(hit, iota((16, LANES), 0) + 1, 0), axis=0, keepdims=True) - 1
        cell = jnp.sum(jnp.where(hit, cells, 0), axis=0, keepdims=True)
        landing[8 * r : 8 * r + 1, :] = number
        landing[8 * r + 1 : 8 * r + 2, :] = jnp.where(number >= 0, cell, -1)
        wide = jnp.broadcast_to(slot - 1, (COLS, LANES))
        first_index, heading, target = hits[r]
        own_first = first_index == wide
        own_second = (heading == 0) & (target == wide)
        from_left = (heading == 2) & (target == roll_cells(wide, -1))
        if r == 1:
            _, above, aim = hits[0]
            straight = (above == 1) & (aim == wide)
            slant = (above == 3) & (aim == roll_cells(wide, -1))
            back = (above == 4) & (aim == roll_cells(wide, 1))
        info = jnp.where(lane == LIVE + 7, slot.astype(jnp.float32), which.astype(jnp.float32))
        for j in range(7):
            base = (r * 8 + j) * COLS
            f = on_first[base : base + COLS, :]
            s = on_second[base : base + COLS, :]
            total = jnp.where(own_first, f, 0.0) + jnp.where(own_second, s, 0.0)
            right = jnp.where(from_left, s, 0.0)
            if r == 1:
                u = on_second[j * COLS : (j + 1) * COLS, :]
                total = total + jnp.where(straight, u, 0.0)
                right = right + jnp.where(slant, u, 0.0)
                total = total + roll_cells(jnp.where(back, u, 0.0), -1)
            total = total + roll_cells(right, 1)
            info = jnp.where(lane == LIVE + j, jnp.sum(total, axis=1, keepdims=True), info)
        infos[r] = info

    turn = lax.rem(lax.axis_index("blade"), 2)
    for out, row in ((to_near, 1 - turn), (to_far, turn)):
        n = jnp.where(row == 1, counted[1], counted[0])
        lists = [pairs[k, row] for k in range(2)]
        for j in range(COMPS):
            value = packed(j, particles[j, row], lists, jnp.broadcast_to(n, (COLS, LANES)), infos[row])
            out[j * COLS : (j + 1) * COLS, :] = value


def edge_terms(
    got_near, got_far, sent_near, sent_far, infos, near_in, far_in, to_far, to_near, edges, edge_first, edge_second
):
    to_near[0:EDGE, :] = near_in[0:EDGE, :]
    to_far[0:EDGE, :] = far_in[0:EDGE, :]
    odd = lax.rem(lax.axis_index("span"), 2) == 1
    west = jnp.where(odd, got_near[...], got_far[...])
    east = jnp.where(odd, got_far[...], got_near[...])
    west_own = jnp.where(odd, sent_near[...], sent_far[...])
    east_own = jnp.where(odd, sent_far[...], sent_near[...])
    for k, side in enumerate((west, west_own, east_own, east)):
        for r in range(2):
            edges[pl.ds(4 * r + k, 12, stride=8), :] = side[r * 12 : r * 12 + 12]
    tile = [edges[j * 8 : j * 8 + 8, :] for j in range(COMPS)]
    first_index, second_index = unpacked(tile[:8])
    heading = second_index // LANES
    target = lax.rem(second_index, LANES)
    spot = iota((8, LANES), 0)
    lane = iota((8, LANES), 1)
    even = lax.rem(spot, 2) == 0
    listed = lane < lane_of(tile[8], 0).astype(jnp.int32)
    listed = listed & (
        ((heading == 2) & even)
        | ((heading == 3) & even & (spot < 4))
        | ((heading == 4) & ~even & (spot < 4))
    )
    first = [pick(t, first_index) for t in tile]
    second = []
    for t in tile:
        beside = pick(roll_cells(t, -1), target)
        below = pick(jnp.where(even, roll_cells(t, -5), roll_cells(t, -3)), target)
        second.append(jnp.where(heading == 2, beside, below))
    row_shift, col_shift = shifts(heading)
    f, s = pair_terms(first, second, row_shift, col_shift, listed)
    keep(edge_first, 0, f)
    keep(edge_second, 0, s)

    slots = [[lane_of(infos[r, c : c + 1, :], 7).astype(jnp.int32) for c in (0, COLS - 1)] for r in range(2)]

    def at_spots(*choices):
        value = jnp.zeros((8, LANES), jnp.int32)
        for k, slot in choices:
            value = jnp.where(spot == k, slot, value)
        return value - 1

    mine = first_index == at_spots((1, slots[0][0]), (2, slots[0][1]), (6, slots[1][1]))
    beside = (heading == 2) & (target == at_spots((0, slots[0][0]), (4, slots[1][0])))
    below = (heading != 2) & (target == at_spots((0, slots[1][0]), (3, slots[1][1])))
    sums = [jnp.zeros((8, LANES), jnp.float32)] * 3
    for j in range(7):
        for k, (hit, term) in enumerate(((mine, f[j]), (beside, s[j]), (below, s[j]))):
            total = jnp.sum(jnp.where(hit, term, 0.0), axis=1, keepdims=True)
            sums[k] = jnp.where(lane == LIVE + j, total, sums[k])
    fixes = (
        (sums[0][1:2] + sums[1][0:1], sums[0][2:3]),
        (sums[1][4:5] + sums[2][0:1], sums[0][6:7] + sums[2][3:4]),
    )
    turn = lax.rem(lax.axis_index("blade"), 2)
    for out, row in ((to_near, 1 - turn), (to_far, turn)):
        low = row == 1
        for k, c in enumerate((0, COLS - 1)):
            at = 9 * COLS + c
            out[at : at + 1, :] += jnp.where(low, fixes[1][k], fixes[0][k])
        out[EDGE : EDGE + 12, :] = jnp.where(low, east[12:24], east[0:12])
        out[EDGE + 12 : EDGE + 24, :] = jnp.where(low, west[12:24], west[0:12])


def own_sums(
    particles, pairs, count, on_first, on_second, edges, edge_first, edge_second,
    ext_in, sums, ext, first_low, lists_low, by_source0, by_source1,
):
    ext[...] = ext_in[...]
    sizes = (40, 16)
    for ref, size in ((by_source0, 40), (by_source1, 16)):
        ref[0:size, :] = jnp.zeros((size, LANES), jnp.float32)
        ref[33 * size : 34 * size, :] = jnp.zeros((size, LANES), jnp.float32)
    blank = jnp.zeros((8, LANES), jnp.float32)
    for r, (ref, headings) in enumerate(((by_source0, (0, 1, 2, 3, 4)), (by_source1, (0, 2)))):

        def source(c, _, r=r, ref=ref, headings=headings):
            f = on_first[pl.ds(r * 8 * COLS + c, 8, stride=COLS), :]
            s = on_second[pl.ds(r * 8 * COLS + c, 8, stride=COLS), :]
            second_row = pairs[1, r, pl.ds(c, 1), :]
            heading = second_row // LANES
            left = jnp.concatenate(
                [jnp.concatenate([f if d == 0 else blank, jnp.where(heading == d, s, 0.0)], 1) for d in headings],
                0,
            )
            out = spread(left, pairs[0, r, pl.ds(c, 1), :], lax.rem(second_row, LANES))
            size = sizes[r]
            ref[pl.ds(pl.multiple_of((c + 1) * size, 8), size), :] = out
            return 0

        lax.fori_loop(0, COLS, source, 0, unroll=32)
    tile = [edges[j * 8 : j * 8 + 8, :] for j in range(COMPS)]
    first_index, second_index = unpacked(tile[:8])
    heading = second_index // LANES
    target = lax.rem(second_index, LANES)
    for k in (0, 1, 2, 3, 4, 6):
        f = edge_first[pl.ds(k, 8, stride=8), :]
        s = edge_second[pl.ds(k, 8, stride=8), :]
        aim = heading[k : k + 1]
        left = jnp.concatenate(
            [
                jnp.concatenate([f, blank], 1),
                jnp.concatenate([blank, jnp.where(aim == 2, s, 0.0)], 1),
                jnp.concatenate([blank, jnp.where(aim == 2, 0.0, s)], 1),
                jnp.zeros((8, 2 * LANES), jnp.float32),
            ],
            0,
        )
        out = spread(left, first_index[k : k + 1], target[k : k + 1])
        if k == 0:
            by_source0[16:24, :] = out[8:16]
            by_source0[24:32, :] = out[16:24]
        elif k == 1:
            by_source0[40:48, :] += out[0:8]
        elif k == 2:
            by_source0[32 * 40 : 32 * 40 + 8, :] += out[0:8]
        elif k == 3:
            by_source0[33 * 40 + 32 : 33 * 40 + 40, :] = out[16:24]
        elif k == 4:
            by_source1[8:16, :] = out[8:16]
        else:
            by_source1[32 * 16 : 32 * 16 + 8, :] += out[0:8]

    def column(ref, size, tile_at, shift, j):
        return ref[pl.ds((1 + shift) * size + tile_at * 8 + j, COLS, stride=size), :]

    for j in range(7):
        sums[0, j] = column(by_source0, 40, 0, 0, j) + column(by_source0, 40, 2, -1, j)
        total = column(by_source1, 16, 0, 0, j) + column(by_source1, 16, 1, -1, j)
        total = total + column(by_source0, 40, 1, 0, j) + column(by_source0, 40, 3, -1, j)
        sums[1, j] = total + column(by_source0, 40, 4, 1, j)

    for r in range(2):
        for j in range(COMPS):
            for k, at in ((3, 40), (0, 41), (1, 42), (0, 7)):
                ext[j, r, at : at + 1, :] = tile[j][4 * r + k : 4 * r + k + 1]
    rows = jnp.concatenate([pairs[0, 1], first_index[7:8], first_index[4:5], jnp.zeros((6, LANES), jnp.int32)], 0)
    seconds = jnp.concatenate([pairs[1, 1], second_index[7:8], second_index[4:5], jnp.zeros((6, LANES), jnp.int32)], 0)
    edge_count = lane_of(tile[8], 0).astype(jnp.int32)
    n = jnp.concatenate(
        [to_column(count[1:2, :], COLS), edge_count[7:8], edge_count[4:5], jnp.zeros((6, 1), jnp.int32)], 0
    )
    lists_low[0] = rows
    lists_low[1] = jnp.where(iota((SLAB, LANES), 1) < n, seconds // LANES, -1)
    lists_low[2] = lax.rem(seconds, LANES)
    for j in range(COMPS):
        first_low[j] = pick(ext[j, 1, BASE : BASE + SLAB, :], rows)


def surround(around, source):
    zeros = jnp.zeros((8, LANES), jnp.float32)
    for j in range(COMPS):
        main = source[j * COLS : (j + 1) * COLS, :]
        right = source[EDGE + j : EDGE + j + 1, :]
        left = source[EDGE + 12 + j : EDGE + 13 + j, :]
        around[j, 40:48, :] = zeros
        around[j, 8:40, :] = main
        around[j, 40:41, :] = right
        around[j, 41:42, :] = left
        around[j, 42:43, :] = main[0:1]
        around[j, 7:8, :] = left


def row_terms(first, others, heading, target):
    second = []
    for j in range(COMPS):
        value = None
        for d in (1, 3, 4):
            got = pick(others(j, col_steps[d]), target)
            value = got if value is None else jnp.where(heading == d, got, value)
        second.append(value)
    listed = (heading == 1) | (heading == 3) | (heading == 4)
    _, col_shift = shifts(heading)
    return pair_terms(first, second, 1.0, col_shift, listed)


def finish(side, info, state, leaving, totals, ext, stays, landing, write):
    slot = lane_of(info, 7).astype(jnp.int32)
    which = lane_of(info, 8).astype(jnp.int32)
    leaves = slot > 0
    leaving = [t + lane_of(info, j) for j, t in enumerate(leaving)]
    at_slot = jnp.broadcast_to(jnp.maximum(slot - 1, 0), (COLS, LANES))
    moved = stepped([pick(v, at_slot) for v in state], leaving, leaves)
    moved[0] = moved[0] + (-1.0 if side == 0 else 1.0)
    match = (which == landing[8 * side : 8 * side + 1, :]) & leaves
    rows = stepped([ext[j, side, BASE : BASE + COLS, :] for j in range(COMPS)], totals, stays[side] > 0)
    lands = iota((COLS, LANES), 0) == landing[8 * side + 1 : 8 * side + 2, :]
    for j in range(COMPS):
        value = jnp.sum(jnp.where(match, moved[j], 0.0), axis=0, keepdims=True)
        write(side, j, jnp.where(lands, value, jnp.where(stays[side] == 1, 0.0, rows[j])))


def from_behind(source, sums, ext, stays, landing, write, around, terms, indices, by_source):
    surround(around, source)
    lane = iota((SLAB, LANES), 1)
    rows = [around[j, BASE : BASE + SLAB, :] for j in range(COMPS)]
    firsts, seconds = unpacked(rows[:8])
    heading = jnp.where(lane < lane_of(rows[8], 0).astype(jnp.int32), seconds // LANES, -1)
    target = lax.rem(seconds, LANES)
    first = [pick(v, firsts) for v in rows]
    f, s = row_terms(first, lambda j, k: ext[j, 0, BASE + k : BASE + k + SLAB, :], heading, target)
    keep(terms, 0, s)
    indices[0] = heading
    indices[1] = target
    for c in range(SOURCES):
        term = terms[pl.ds(c, 8, stride=SLAB), :]
        aim = indices[0, c : c + 1, :]
        left = jnp.concatenate([jnp.where(aim == d, term, 0.0) for d in (1, 3, 4)], 0)
        by_source[(c + 1) * 24 : (c + 2) * 24, :] = spread(left, indices[1, c : c + 1, :])
    by_source[0:24, :] = by_source[34 * 24 : 35 * 24, :]
    info = rows[9][:COLS]
    hit = firsts[:COLS] == lane_of(info, 7).astype(jnp.int32) - 1
    leaving = [jnp.sum(jnp.where(hit, f[j][:COLS], 0.0), axis=1, keepdims=True) for j in range(7)]
    totals = []
    for j in range(7):
        total = sums[0, j]
        for k, shift in ((0, 0), (1, -1), (2, 1)):
            total = total + by_source[pl.ds((1 + shift) * 24 + k * 8 + j, COLS, stride=24), :]
        totals.append(total)
    state = [v[:COLS] for v in rows]
    finish(0, info, state, leaving, totals, ext, stays, landing, write)


def from_ahead(source, sums, ext, first_low, lists_low, stays, landing, write, around, terms, by_source):
    surround(around, source)
    heading, target = lists_low[1], lists_low[2]
    first = [first_low[j] for j in range(COMPS)]
    f, s = row_terms(first, lambda j, k: around[j, BASE + k : BASE + k + SLAB, :], heading, target)
    keep(terms, 0, f)
    for c in range(COLS):
        by_source[c * 8 : c * 8 + 8, :] = spread(terms[pl.ds(c, 8, stride=SLAB), :], lists_low[0, c : c + 1, :])
    info = around[9, BASE : BASE + COLS, :]
    wide = jnp.broadcast_to(lane_of(info, 7).astype(jnp.int32) - 1, (COLS, LANES))
    wide = jnp.concatenate([wide, jnp.full((8, LANES), -1, jnp.int32)], 0)
    up = jnp.where(iota((SLAB, LANES), 0) == 33, wide[0:1], roll_cells(wide, -1))
    straight = (heading == 1) & (target == wide)
    slanting = (heading == 3) & (target == up)
    back = (heading == 4) & (target == roll_cells(wide, 1))
    first_cell = iota((COLS, LANES), 0) == 0
    leaving = []
    for j in range(7):
        slant = jnp.where(slanting, s[j], 0.0)
        slant = jnp.where(first_cell, slant[33:34], roll_cells(slant, 1)[:COLS])
        total = jnp.where(straight, s[j], 0.0)[:COLS] + slant
        total = total + roll_cells(jnp.where(back, s[j], 0.0), -1)[:COLS]
        leaving.append(jnp.sum(total, axis=1, keepdims=True))
    totals = [sums[1, j] + by_source[pl.ds(j, COLS, stride=8), :] for j in range(7)]
    state = [around[j, BASE : BASE + COLS, :] for j in range(COMPS)]
    finish(1, info, state, leaving, totals, ext, stays, landing, write)


def far_row(far, sums, ext, first_low, lists_low, stays, landing, half, around, terms, indices, by_source):
    odd = lax.rem(lax.axis_index("blade"), 2) == 1

    def write(side, j, value):
        half[j] = value

    @pl.when(odd)
    def _():
        from_ahead(far, sums, ext, first_low, lists_low, stays, landing, write, around, terms, by_source)

    @pl.when(jnp.logical_not(odd))
    def _():
        from_behind(far, sums, ext, stays, landing, write, around, terms, indices, by_source)


def near_row(near, half, sums, ext, first_low, lists_low, stays, landing, out, around, terms, indices, by_source):
    odd = lax.rem(lax.axis_index("blade"), 2) == 1

    def write(side, j, value):
        out[j, side] = value
        out[j, 1 - side] = half[j]

    @pl.when(odd)
    def _():
        from_behind(near, sums, ext, stays, landing, write, around, terms, indices, by_source)

    @pl.when(jnp.logical_not(odd))
    def _():
        from_ahead(near, sums, ext, first_low, lists_low, stays, landing, write, around, terms, by_source)


def swapped(block, axis, start):
    pairs = []
    for i in range(start, lax.axis_size(axis) - 1, 2):
        pairs += [(i, i + 1), (i + 1, i)]
    return lax.ppermute(block, axis, pairs)


vmem = pl.BlockSpec(memory_space=pltpu.VMEM)
smem = pl.BlockSpec(memory_space=pltpu.SMEM)
hbm = pl.BlockSpec(memory_space=pltpu.HBM)
params = pltpu.CompilerParams(vmem_limit_bytes=24 * 1024 * 1024)


def shape(*dims, dtype=jnp.float32):
    return jax.ShapeDtypeStruct(dims, dtype)


def buffer(*dims, dtype=jnp.float32):
    return pltpu.VMEM(dims, dtype)


def body(particles, filled, contact_pairs, contact_count, movers_out, movers_in, move_count):
    ints = jnp.int32
    far, near = pl.pallas_call(
        pack_columns,
        in_specs=[hbm] * 3,
        out_specs=[vmem] * 2,
        out_shape=[shape(24, LANES)] * 2,
        scratch_shapes=[
            buffer(COMPS, 2, 8, LANES),
            buffer(COMPS, 2, 8, LANES),
            buffer(2, 2, 8, LANES, dtype=ints),
            buffer(2, 2, 8, LANES, dtype=ints),
            buffer(2, COLS, dtype=ints),
            pltpu.SemaphoreType.DMA((5,)),
        ],
        compiler_params=params,
        name="pack_columns",
    )(*(pltpu.with_memory_space_constraint(x, pltpu.HBM) for x in (particles, contact_pairs, contact_count)))
    got_far = swapped(far, "span", 1)
    got_near = swapped(near, "span", 0)
    on_first, on_second, to_near, to_far, ext, infos, stays, landing = pl.pallas_call(
        inner_terms,
        in_specs=[vmem] * 6 + [smem],
        out_specs=[vmem] * 8,
        out_shape=[
            shape(16 * COLS, LANES),
            shape(16 * COLS, LANES),
            shape(PAYLOAD, LANES),
            shape(PAYLOAD, LANES),
            shape(COMPS, 2, EXT, LANES),
            shape(2, COLS, LANES),
            shape(2, COLS, LANES, dtype=ints),
            shape(16, LANES, dtype=ints),
        ],
        compiler_params=params,
        name="inner_terms",
    )(particles, contact_pairs, contact_count, filled, movers_out, movers_in, move_count)
    to_far, to_near, edges, edge_first, edge_second = pl.pallas_call(
        edge_terms,
        in_specs=[vmem] * 7,
        out_specs=[vmem] * 5,
        out_shape=[
            shape(PAYLOAD, LANES),
            shape(PAYLOAD, LANES),
            shape(96, LANES),
            shape(64, LANES),
            shape(64, LANES),
        ],
        compiler_params=params,
        name="edge_terms",
    )(got_near, got_far, near, far, infos, to_near, to_far)
    row_far = swapped(to_far, "blade", 1)
    row_near = swapped(to_near, "blade", 0)
    sums, ext, first_low, lists_low = pl.pallas_call(
        own_sums,
        in_specs=[vmem] * 9,
        out_specs=[vmem] * 4,
        out_shape=[
            shape(2, 7, COLS, LANES),
            shape(COMPS, 2, EXT, LANES),
            shape(COMPS, SLAB, LANES),
            shape(3, SLAB, LANES, dtype=ints),
        ],
        scratch_shapes=[buffer(34 * 40, LANES), buffer(34 * 16, LANES)],
        compiler_params=params,
        name="own_sums",
    )(particles, contact_pairs, contact_count, on_first, on_second, edges, edge_first, edge_second, ext)
    own = (sums, ext, first_low, lists_low, stays, landing)
    scratch = [
        buffer(COMPS, EXT, LANES),
        buffer(8 * SLAB, LANES),
        buffer(2, SLAB, LANES, dtype=ints),
        buffer(35 * 24, LANES),
    ]
    half = pl.pallas_call(
        far_row,
        in_specs=[vmem] * 7,
        out_specs=vmem,
        out_shape=shape(COMPS, COLS, LANES),
        scratch_shapes=scratch,
        compiler_params=params,
        name="far_row",
    )(row_far, *own)
    return pl.pallas_call(
        near_row,
        in_specs=[vmem] * 8,
        out_specs=vmem,
        out_shape=shape(COMPS, 2, COLS, LANES),
        scratch_shapes=scratch,
        compiler_params=params,
        name="near_row",
    )(row_near, half, *own)


def solution(mesh):
    return jax.shard_map(
        body,
        mesh=mesh,
        in_specs=(
            P(None, "blade", "span", None),
            P("blade", "span"),
            P(None, "blade", "span", None),
            P("blade", "span"),
            P(None, None, "blade", "span"),
            P(None, None, "blade", "span"),
            P(None, "blade", "span"),
        ),
        out_specs=P(None, "blade", "span", None),
        check_vma=False,
    )
```

```python
import jax
import jax.numpy as jnp
from jax import lax
from jax.experimental import pallas as pl
from jax.experimental.pallas import tpu as pltpu
from jax.sharding import PartitionSpec as P

spring = 4.0
normal_damp = 0.5
tangent_damp = 0.3
conduct = 40.0
timestep = 0.05
density = 100.0
gravity = 9.81
soft_len = 0.05

COMPS = 11
LANES = 128
LIVE = 96
COLS = 32
SLAB = 40
EXT = 56
BASE = 8
SOURCES = 34
EDGE = COMPS * COLS
PAYLOAD = EDGE + 24
row_steps = (0, 1, 0, 1, 1)
col_steps = (0, 0, 1, 1, -1)


def iota(shape, dim):
    return lax.broadcasted_iota(jnp.int32, shape, dim)


def pick(values, index):
    return jnp.take_along_axis(values, index, axis=1, mode="promise_in_bounds")


def to_column(row, size):
    n = row.shape[1]
    spread = jnp.where(iota((size, n), 0) == iota((size, n), 1), row, 0)
    return jnp.sum(spread, axis=1, keepdims=True)


def cross(a, b):
    return (
        a[1] * b[2] - a[2] * b[1],
        a[2] * b[0] - a[0] * b[2],
        a[0] * b[1] - a[1] * b[0],
    )


def pair_terms(first, second, row_shift, col_shift, listed):
    gap = (second[0] + row_shift - first[0], second[1] + col_shift - first[1], second[2] - first[2])
    dist = jnp.sqrt(gap[0] * gap[0] + gap[1] * gap[1] + gap[2] * gap[2] + soft_len * soft_len)
    inverse = 1.0 / dist
    n = tuple(g * inverse for g in gap)
    r1, r2 = first[9], second[9]
    intersection = r1 + r2 - dist
    spin = tuple(r1 * first[6 + i] + r2 * second[6 + i] for i in range(3))
    turn = cross(spin, n)
    w = tuple(second[3 + i] - first[3 + i] - turn[i] for i in range(3))
    u = w[0] * n[0] + w[1] * n[1] + w[2] * n[2]
    fric = tuple(tangent_damp * (w[i] - u * n[i]) for i in range(3))
    push = normal_damp * u - spring * intersection
    force = tuple(push * n[i] + fric[i] for i in range(3))
    torque = cross(n, fric)
    denom = jnp.where(listed, r1 + r2, 1.0)
    heat = 2.0 * conduct * r1 * r2 / denom * (second[10] - first[10])
    on_first = [*force, *(r1 * t for t in torque), heat]
    on_second = [*(-f for f in force), *(r2 * t for t in torque), -heat]
    return (
        [jnp.where(listed, t, 0.0) for t in on_first],
        [jnp.where(listed, t, 0.0) for t in on_second],
    )


def stepped(state, totals, live):
    r = state[9] + jnp.where(live, 0.0, 1.0)
    mass = density * r * r * r
    per_mass = timestep / mass
    per_inertia = timestep / (0.4 * mass * r * r)
    v = [state[3] + per_mass * totals[0], state[4] + per_mass * totals[1]]
    v.append(state[5] + per_mass * totals[2] - timestep * gravity)
    spin = [state[6 + i] + per_inertia * totals[3 + i] for i in range(3)]
    x = [state[i] + timestep * v[i] for i in range(3)]
    warmth = state[10] + per_mass * totals[6]
    return [jnp.where(live, t, 0.0) for t in [*x, *v, *spin, state[9], warmth]]


def shifts(heading):
    row_shift = jnp.where((heading == 0) | (heading == 2), 0.0, 1.0)
    col_shift = jnp.where(
        (heading == 2) | (heading == 3), 1.0, jnp.where(heading == 4, -1.0, 0.0)
    )
    return row_shift, col_shift


def keep(ref, base, terms):
    n = terms[0].shape[0]
    for j in range(7):
        ref[base + j * n : base + (j + 1) * n, :] = terms[j]
    ref[base + 7 * n : base + 8 * n, :] = jnp.zeros((n, LANES), jnp.float32)


def halves(x):
    high = x.astype(jnp.bfloat16).astype(jnp.float32)
    return jnp.concatenate([high, x - high], 0).astype(jnp.bfloat16)


def one_hot(index_row):
    hot = iota((LANES, LANES), 0) == index_row
    return jnp.where(hot, 1.0, 0.0).astype(jnp.bfloat16)


def spread(left, *index_rows):
    hot = jnp.concatenate([one_hot(row) for row in index_rows], 1)
    out = lax.dot_general(
        halves(left), hot, (((1,), (1,)), ((), ())), preferred_element_type=jnp.float32
    )
    rows = left.shape[0]
    return out[:rows] + out[rows:]


def packed(j, value, lists, count, info):
    lane = iota(value.shape, 1)
    if j < 8:
        extra = lists[j // 4].astype(jnp.float32)
        if j % 4 != 3:
            extra = pltpu.roll(extra, LIVE - 32 * (j % 4), 1)
    elif j == 8:
        extra = count.astype(jnp.float32)
    elif j == 9 and info is not None:
        extra = info
    else:
        return value
    return jnp.where(lane < LIVE, value, extra)


def unpacked(rows):
    lane = iota(rows[0].shape, 1)
    lists = []
    for half in range(2):
        value = rows[half * 4 + 3]
        for k in range(3):
            moved = pltpu.roll(rows[half * 4 + k], 32 * k + 32, 1)
            value = jnp.where(lane // 32 == k, moved, value)
        lists.append(value.astype(jnp.int32))
    return lists


def lane_of(value, k):
    return value[:, LIVE + k : LIVE + k + 1]


def pack_columns(particles, pairs, count, far, near, p_west, p_east, c_west, c_east, n_all, sems):
    last = COLS - 1
    copies = [
        pltpu.make_async_copy(particles.at[:, :, 0:1, :], p_west, sems.at[0]),
        pltpu.make_async_copy(particles.at[:, :, last:COLS, :], p_east, sems.at[1]),
        pltpu.make_async_copy(pairs.at[:, :, 0:1, :], c_west, sems.at[2]),
        pltpu.make_async_copy(pairs.at[:, :, last:COLS, :], c_east, sems.at[3]),
        pltpu.make_async_copy(count, n_all, sems.at[4]),
    ]
    for copy in copies:
        copy.start()
    near[...] = jnp.zeros(near.shape, jnp.float32)
    far[...] = jnp.zeros(far.shape, jnp.float32)
    odd = lax.rem(lax.axis_index("span"), 2) == 1
    for copy in copies:
        copy.wait()
    for r in range(2):
        n_row = n_all[r : r + 1, :]
        sides = []
        for p, c, at, cell in ((p_west, c_west, 0, 0), (p_east, c_east, 0, COLS - 1)):
            n = jnp.sum(jnp.where(iota((1, COLS), 1) == cell, n_row, 0), axis=1, keepdims=True)
            lists = [c[k, r, at : at + 1, :] for k in range(2)]
            sides.append([packed(j, p[j, r, at : at + 1, :], lists, n, None) for j in range(COMPS)])
        for j in range(COMPS):
            west, east = sides[0][j], sides[1][j]
            row = r * 12 + j
            near[row : row + 1, :] = jnp.where(odd, west, east)
            far[row : row + 1, :] = jnp.where(odd, east, west)


def leavers(movers, counts, row):
    direction = 1 - row
    cells = lax.rem(movers[direction, 0], COLS)
    slots = movers[direction, 1]
    n = cells.shape[1]
    number = iota((COLS, n), 1)
    here = (iota((COLS, n), 0) == cells) & (number < counts[direction, 0, 0])
    slot = jnp.sum(jnp.where(here, slots + 1, 0), axis=1, keepdims=True)
    which = jnp.sum(jnp.where(here, number, 0), axis=1, keepdims=True)
    return slot, which


def roll_cells(value, step):
    return pltpu.roll(value, step % value.shape[0], 0)


def inner_terms(
    particles, pairs, count, filled, movers, arrivals, counts,
    on_first, on_second, to_near, to_far, ext, infos, stays, landing,
):
    lane = iota((COLS, LANES), 1)
    column = iota((COLS, LANES), 0)
    zeros = jnp.zeros((8, LANES), jnp.float32)
    for r in range(2):
        for j in range(COMPS):
            ext[j, r, 0:8, :] = zeros
            ext[j, r, 40:48, :] = zeros
            ext[j, r, 8:40, :] = particles[j, r]
    counted = [to_column(count[r : r + 1, :], COLS) for r in range(2)]
    hits = []
    for r in range(2):
        headings = (0, 1, 2, 3, 4) if r == 0 else (0, 2)
        first_index = pairs[0, r]
        heading = pairs[1, r] // LANES
        target = lax.rem(pairs[1, r], LANES)
        outside = (column == COLS - 1) & ((heading == 2) | (heading == 3)) | (column == 0) & (heading == 4)
        listed = (lane < counted[r]) & ~outside
        if r == 1:
            listed = listed & ((heading == 0) | (heading == 2))
        row_shift, col_shift = shifts(heading)
        for g in range(0, COLS, 8):
            rows = slice(g, g + 8)
            first = [pick(particles[j, r, rows, :], first_index[rows]) for j in range(COMPS)]
            second = []
            for j in range(COMPS):
                value = None
                for d in headings:
                    at = BASE + col_steps[d] + g
                    got = pick(ext[j, r + row_steps[d], at : at + 8, :], target[rows])
                    value = got if value is None else jnp.where(heading[rows] == d, got, value)
                second.append(value)
            f, s = pair_terms(first, second, row_shift[rows], col_shift[rows], listed[rows])
            for ref, terms in ((on_first, f), (on_second, s)):
                for j in range(7):
                    at = (r * 8 + j) * COLS + g
                    ref[at : at + 8, :] = terms[j]
        for ref in (on_first, on_second):
            at = (r * 8 + 7) * COLS
            ref[at : at + COLS, :] = jnp.zeros((COLS, LANES), jnp.float32)
        hits.append((first_index, heading, target))

    for r in range(2):
        slot, which = leavers(movers, counts, r)
        live = lane < to_column(filled[r : r + 1, :], COLS)
        stays[r] = jnp.where(live, jnp.where(lane != slot - 1, 2, 1), 0)
        cells = to_column(lax.rem(arrivals[r, 0], COLS), 16)
        slots = to_column(arrivals[r, 1], 16)
        hit = slots == iota((16, LANES), 1)
        number = jnp.sum(jnp.where(hit, iota((16, LANES), 0) + 1, 0), axis=0, keepdims=True) - 1
        cell = jnp.sum(jnp.where(hit, cells, 0), axis=0, keepdims=True)
        landing[8 * r : 8 * r + 1, :] = number
        landing[8 * r + 1 : 8 * r + 2, :] = jnp.where(number >= 0, cell, -1)
        wide = jnp.broadcast_to(slot - 1, (COLS, LANES))
        first_index, heading, target = hits[r]
        own_first = first_index == wide
        own_second = (heading == 0) & (target == wide)
        from_left = (heading == 2) & (target == roll_cells(wide, -1))
        if r == 1:
            _, above, aim = hits[0]
            straight = (above == 1) & (aim == wide)
            slant = (above == 3) & (aim == roll_cells(wide, -1))
            back = (above == 4) & (aim == roll_cells(wide, 1))
        info = jnp.where(lane == LIVE + 7, slot.astype(jnp.float32), which.astype(jnp.float32))
        for j in range(7):
            base = (r * 8 + j) * COLS
            f = on_first[base : base + COLS, :]
            s = on_second[base : base + COLS, :]
            total = jnp.where(own_first, f, 0.0) + jnp.where(own_second, s, 0.0)
            right = jnp.where(from_left, s, 0.0)
            if r == 1:
                u = on_second[j * COLS : (j + 1) * COLS, :]
                total = total + jnp.where(straight, u, 0.0)
                right = right + jnp.where(slant, u, 0.0)
                total = total + roll_cells(jnp.where(back, u, 0.0), -1)
            total = total + roll_cells(right, 1)
            info = jnp.where(lane == LIVE + j, jnp.sum(total, axis=1, keepdims=True), info)
        infos[r] = info

    turn = lax.rem(lax.axis_index("blade"), 2)
    for out, row in ((to_near, 1 - turn), (to_far, turn)):
        n = jnp.where(row == 1, counted[1], counted[0])
        lists = [pairs[k, row] for k in range(2)]
        for j in range(COMPS):
            value = packed(j, particles[j, row], lists, jnp.broadcast_to(n, (COLS, LANES)), infos[row])
            out[j * COLS : (j + 1) * COLS, :] = value


def edge_terms(
    got_near, got_far, sent_near, sent_far, infos, near_in, far_in, to_far, to_near, edges, edge_first, edge_second
):
    to_near[0:EDGE, :] = near_in[0:EDGE, :]
    to_far[0:EDGE, :] = far_in[0:EDGE, :]
    odd = lax.rem(lax.axis_index("span"), 2) == 1
    west = jnp.where(odd, got_near[...], got_far[...])
    east = jnp.where(odd, got_far[...], got_near[...])
    west_own = jnp.where(odd, sent_near[...], sent_far[...])
    east_own = jnp.where(odd, sent_far[...], sent_near[...])
    for k, side in enumerate((west, west_own, east_own, east)):
        for r in range(2):
            edges[pl.ds(4 * r + k, 12, stride=8), :] = side[r * 12 : r * 12 + 12]
    tile = [edges[j * 8 : j * 8 + 8, :] for j in range(COMPS)]
    first_index, second_index = unpacked(tile[:8])
    heading = second_index // LANES
    target = lax.rem(second_index, LANES)
    spot = iota((8, LANES), 0)
    lane = iota((8, LANES), 1)
    even = lax.rem(spot, 2) == 0
    listed = lane < lane_of(tile[8], 0).astype(jnp.int32)
    listed = listed & (
        ((heading == 2) & even)
        | ((heading == 3) & even & (spot < 4))
        | ((heading == 4) & ~even & (spot < 4))
    )
    first = [pick(t, first_index) for t in tile]
    second = []
    for t in tile:
        beside = pick(roll_cells(t, -1), target)
        below = pick(jnp.where(even, roll_cells(t, -5), roll_cells(t, -3)), target)
        second.append(jnp.where(heading == 2, beside, below))
    row_shift, col_shift = shifts(heading)
    f, s = pair_terms(first, second, row_shift, col_shift, listed)
    keep(edge_first, 0, f)
    keep(edge_second, 0, s)

    slots = [[lane_of(infos[r, c : c + 1, :], 7).astype(jnp.int32) for c in (0, COLS - 1)] for r in range(2)]

    def at_spots(*choices):
        value = jnp.zeros((8, LANES), jnp.int32)
        for k, slot in choices:
            value = jnp.where(spot == k, slot, value)
        return value - 1

    mine = first_index == at_spots((1, slots[0][0]), (2, slots[0][1]), (6, slots[1][1]))
    beside = (heading == 2) & (target == at_spots((0, slots[0][0]), (4, slots[1][0])))
    below = (heading != 2) & (target == at_spots((0, slots[1][0]), (3, slots[1][1])))
    sums = [jnp.zeros((8, LANES), jnp.float32)] * 3
    for j in range(7):
        for k, (hit, term) in enumerate(((mine, f[j]), (beside, s[j]), (below, s[j]))):
            total = jnp.sum(jnp.where(hit, term, 0.0), axis=1, keepdims=True)
            sums[k] = jnp.where(lane == LIVE + j, total, sums[k])
    fixes = (
        (sums[0][1:2] + sums[1][0:1], sums[0][2:3]),
        (sums[1][4:5] + sums[2][0:1], sums[0][6:7] + sums[2][3:4]),
    )
    turn = lax.rem(lax.axis_index("blade"), 2)
    for out, row in ((to_near, 1 - turn), (to_far, turn)):
        low = row == 1
        for k, c in enumerate((0, COLS - 1)):
            at = 9 * COLS + c
            out[at : at + 1, :] += jnp.where(low, fixes[1][k], fixes[0][k])
        out[EDGE : EDGE + 12, :] = jnp.where(low, east[12:24], east[0:12])
        out[EDGE + 12 : EDGE + 24, :] = jnp.where(low, west[12:24], west[0:12])


def own_sums(
    particles, pairs, count, on_first, on_second, edges, edge_first, edge_second,
    ext_in, sums, ext, first_low, lists_low, by_source0, by_source1,
):
    ext[...] = ext_in[...]
    sizes = (40, 16)
    for ref, size in ((by_source0, 40), (by_source1, 16)):
        ref[0:size, :] = jnp.zeros((size, LANES), jnp.float32)
        ref[33 * size : 34 * size, :] = jnp.zeros((size, LANES), jnp.float32)
    blank = jnp.zeros((8, LANES), jnp.float32)
    for r, (ref, headings) in enumerate(((by_source0, (0, 1, 2, 3, 4)), (by_source1, (0, 2)))):

        def source(c, _, r=r, ref=ref, headings=headings):
            f = on_first[pl.ds(r * 8 * COLS + c, 8, stride=COLS), :]
            s = on_second[pl.ds(r * 8 * COLS + c, 8, stride=COLS), :]
            second_row = pairs[1, r, pl.ds(c, 1), :]
            heading = second_row // LANES
            left = jnp.concatenate(
                [jnp.concatenate([f if d == 0 else blank, jnp.where(heading == d, s, 0.0)], 1) for d in headings],
                0,
            )
            out = spread(left, pairs[0, r, pl.ds(c, 1), :], lax.rem(second_row, LANES))
            size = sizes[r]
            ref[pl.ds(pl.multiple_of((c + 1) * size, 8), size), :] = out
            return 0

        lax.fori_loop(0, COLS, source, 0, unroll=32)
    tile = [edges[j * 8 : j * 8 + 8, :] for j in range(COMPS)]
    first_index, second_index = unpacked(tile[:8])
    heading = second_index // LANES
    target = lax.rem(second_index, LANES)
    for k in (0, 1, 2, 3, 4, 6):
        f = edge_first[pl.ds(k, 8, stride=8), :]
        s = edge_second[pl.ds(k, 8, stride=8), :]
        aim = heading[k : k + 1]
        left = jnp.concatenate(
            [
                jnp.concatenate([f, blank], 1),
                jnp.concatenate([blank, jnp.where(aim == 2, s, 0.0)], 1),
                jnp.concatenate([blank, jnp.where(aim == 2, 0.0, s)], 1),
                jnp.zeros((8, 2 * LANES), jnp.float32),
            ],
            0,
        )
        out = spread(left, first_index[k : k + 1], target[k : k + 1])
        if k == 0:
            by_source0[16:24, :] = out[8:16]
            by_source0[24:32, :] = out[16:24]
        elif k == 1:
            by_source0[40:48, :] += out[0:8]
        elif k == 2:
            by_source0[32 * 40 : 32 * 40 + 8, :] += out[0:8]
        elif k == 3:
            by_source0[33 * 40 + 32 : 33 * 40 + 40, :] = out[16:24]
        elif k == 4:
            by_source1[8:16, :] = out[8:16]
        else:
            by_source1[32 * 16 : 32 * 16 + 8, :] += out[0:8]

    def column(ref, size, tile_at, shift, j):
        return ref[pl.ds((1 + shift) * size + tile_at * 8 + j, COLS, stride=size), :]

    for j in range(7):
        sums[0, j] = column(by_source0, 40, 0, 0, j) + column(by_source0, 40, 2, -1, j)
        total = column(by_source1, 16, 0, 0, j) + column(by_source1, 16, 1, -1, j)
        total = total + column(by_source0, 40, 1, 0, j) + column(by_source0, 40, 3, -1, j)
        sums[1, j] = total + column(by_source0, 40, 4, 1, j)

    for r in range(2):
        for j in range(COMPS):
            for k, at in ((3, 40), (0, 41), (1, 42), (0, 7)):
                ext[j, r, at : at + 1, :] = tile[j][4 * r + k : 4 * r + k + 1]
    rows = jnp.concatenate([pairs[0, 1], first_index[7:8], first_index[4:5], jnp.zeros((6, LANES), jnp.int32)], 0)
    seconds = jnp.concatenate([pairs[1, 1], second_index[7:8], second_index[4:5], jnp.zeros((6, LANES), jnp.int32)], 0)
    edge_count = lane_of(tile[8], 0).astype(jnp.int32)
    n = jnp.concatenate(
        [to_column(count[1:2, :], COLS), edge_count[7:8], edge_count[4:5], jnp.zeros((6, 1), jnp.int32)], 0
    )
    lists_low[0] = rows
    lists_low[1] = jnp.where(iota((SLAB, LANES), 1) < n, seconds // LANES, -1)
    lists_low[2] = lax.rem(seconds, LANES)
    for j in range(COMPS):
        first_low[j] = pick(ext[j, 1, BASE : BASE + SLAB, :], rows)


def surround(around, source):
    zeros = jnp.zeros((8, LANES), jnp.float32)
    for j in range(COMPS):
        main = source[j * COLS : (j + 1) * COLS, :]
        right = source[EDGE + j : EDGE + j + 1, :]
        left = source[EDGE + 12 + j : EDGE + 13 + j, :]
        around[j, 40:48, :] = zeros
        around[j, 8:40, :] = main
        around[j, 40:41, :] = right
        around[j, 41:42, :] = left
        around[j, 42:43, :] = main[0:1]
        around[j, 7:8, :] = left


def row_terms(first, others, heading, target):
    _, col_shift = shifts(heading)
    pieces = []
    for g in range(0, SLAB, 8):
        rows = slice(g, g + 8)
        aim = heading[rows]
        second = []
        for j in range(COMPS):
            value = None
            for d in (1, 3, 4):
                got = pick(others(j, BASE + col_steps[d] + g), target[rows])
                value = got if value is None else jnp.where(aim == d, got, value)
            second.append(value)
        listed = (aim == 1) | (aim == 3) | (aim == 4)
        pieces.append(pair_terms([first(j, rows) for j in range(COMPS)], second, 1.0, col_shift[rows], listed))
    return [[jnp.concatenate([piece[k][j] for piece in pieces], 0) for j in range(7)] for k in range(2)]


def finish(side, info, state, leaving, totals, ext, stays, landing, write):
    slot = lane_of(info, 7).astype(jnp.int32)
    which = lane_of(info, 8).astype(jnp.int32)
    leaves = slot > 0
    leaving = [t + lane_of(info, j) for j, t in enumerate(leaving)]
    at_slot = jnp.broadcast_to(jnp.maximum(slot - 1, 0), (COLS, LANES))
    moved = stepped([pick(v, at_slot) for v in state], leaving, leaves)
    moved[0] = moved[0] + (-1.0 if side == 0 else 1.0)
    match = (which == landing[8 * side : 8 * side + 1, :]) & leaves
    rows = stepped([ext[j, side, BASE : BASE + COLS, :] for j in range(COMPS)], totals, stays[side] > 0)
    lands = iota((COLS, LANES), 0) == landing[8 * side + 1 : 8 * side + 2, :]
    for j in range(COMPS):
        value = jnp.sum(jnp.where(match, moved[j], 0.0), axis=0, keepdims=True)
        write(side, j, jnp.where(lands, value, jnp.where(stays[side] == 1, 0.0, rows[j])))


def from_behind(source, sums, ext, stays, landing, write, around, terms, indices, by_source):
    surround(around, source)
    lane = iota((SLAB, LANES), 1)
    rows = [around[j, BASE : BASE + SLAB, :] for j in range(COMPS)]
    firsts, seconds = unpacked(rows[:8])
    heading = jnp.where(lane < lane_of(rows[8], 0).astype(jnp.int32), seconds // LANES, -1)
    target = lax.rem(seconds, LANES)
    f, s = row_terms(
        lambda j, at: pick(rows[j][at], firsts[at]), lambda j, at: ext[j, 0, at : at + 8, :], heading, target
    )
    keep(terms, 0, s)
    indices[0] = heading
    indices[1] = target
    for c in range(SOURCES):
        term = terms[pl.ds(c, 8, stride=SLAB), :]
        aim = indices[0, c : c + 1, :]
        left = jnp.concatenate([jnp.where(aim == d, term, 0.0) for d in (1, 3, 4)], 0)
        by_source[(c + 1) * 24 : (c + 2) * 24, :] = spread(left, indices[1, c : c + 1, :])
    by_source[0:24, :] = by_source[34 * 24 : 35 * 24, :]
    info = rows[9][:COLS]
    hit = firsts[:COLS] == lane_of(info, 7).astype(jnp.int32) - 1
    leaving = [jnp.sum(jnp.where(hit, f[j][:COLS], 0.0), axis=1, keepdims=True) for j in range(7)]
    totals = []
    for j in range(7):
        total = sums[0, j]
        for k, shift in ((0, 0), (1, -1), (2, 1)):
            total = total + by_source[pl.ds((1 + shift) * 24 + k * 8 + j, COLS, stride=24), :]
        totals.append(total)
    state = [v[:COLS] for v in rows]
    finish(0, info, state, leaving, totals, ext, stays, landing, write)


def from_ahead(source, sums, ext, first_low, lists_low, stays, landing, write, around, terms, by_source):
    surround(around, source)
    heading, target = lists_low[1], lists_low[2]
    f, s = row_terms(
        lambda j, at: first_low[j, at, :], lambda j, at: around[j, at : at + 8, :], heading, target
    )
    keep(terms, 0, f)
    for c in range(COLS):
        by_source[c * 8 : c * 8 + 8, :] = spread(terms[pl.ds(c, 8, stride=SLAB), :], lists_low[0, c : c + 1, :])
    info = around[9, BASE : BASE + COLS, :]
    wide = jnp.broadcast_to(lane_of(info, 7).astype(jnp.int32) - 1, (COLS, LANES))
    wide = jnp.concatenate([wide, jnp.full((8, LANES), -1, jnp.int32)], 0)
    up = jnp.where(iota((SLAB, LANES), 0) == 33, wide[0:1], roll_cells(wide, -1))
    straight = (heading == 1) & (target == wide)
    slanting = (heading == 3) & (target == up)
    back = (heading == 4) & (target == roll_cells(wide, 1))
    first_cell = iota((COLS, LANES), 0) == 0
    leaving = []
    for j in range(7):
        slant = jnp.where(slanting, s[j], 0.0)
        slant = jnp.where(first_cell, slant[33:34], roll_cells(slant, 1)[:COLS])
        total = jnp.where(straight, s[j], 0.0)[:COLS] + slant
        total = total + roll_cells(jnp.where(back, s[j], 0.0), -1)[:COLS]
        leaving.append(jnp.sum(total, axis=1, keepdims=True))
    totals = [sums[1, j] + by_source[pl.ds(j, COLS, stride=8), :] for j in range(7)]
    state = [around[j, BASE : BASE + COLS, :] for j in range(COMPS)]
    finish(1, info, state, leaving, totals, ext, stays, landing, write)


def far_row(far, sums, ext, first_low, lists_low, stays, landing, half, around, terms, indices, by_source):
    odd = lax.rem(lax.axis_index("blade"), 2) == 1

    def write(side, j, value):
        half[j] = value

    @pl.when(odd)
    def _():
        from_ahead(far, sums, ext, first_low, lists_low, stays, landing, write, around, terms, by_source)

    @pl.when(jnp.logical_not(odd))
    def _():
        from_behind(far, sums, ext, stays, landing, write, around, terms, indices, by_source)


def near_row(near, half, sums, ext, first_low, lists_low, stays, landing, out, around, terms, indices, by_source):
    odd = lax.rem(lax.axis_index("blade"), 2) == 1

    def write(side, j, value):
        out[j, side] = value
        out[j, 1 - side] = half[j]

    @pl.when(odd)
    def _():
        from_behind(near, sums, ext, stays, landing, write, around, terms, indices, by_source)

    @pl.when(jnp.logical_not(odd))
    def _():
        from_ahead(near, sums, ext, first_low, lists_low, stays, landing, write, around, terms, by_source)


def swapped(block, axis, start):
    pairs = []
    for i in range(start, lax.axis_size(axis) - 1, 2):
        pairs += [(i, i + 1), (i + 1, i)]
    return lax.ppermute(block, axis, pairs)


vmem = pl.BlockSpec(memory_space=pltpu.VMEM)
smem = pl.BlockSpec(memory_space=pltpu.SMEM)
hbm = pl.BlockSpec(memory_space=pltpu.HBM)
params = pltpu.CompilerParams(vmem_limit_bytes=24 * 1024 * 1024)


def shape(*dims, dtype=jnp.float32):
    return jax.ShapeDtypeStruct(dims, dtype)


def buffer(*dims, dtype=jnp.float32):
    return pltpu.VMEM(dims, dtype)


def body(particles, filled, contact_pairs, contact_count, movers_out, movers_in, move_count):
    ints = jnp.int32
    far, near = pl.pallas_call(
        pack_columns,
        in_specs=[hbm] * 3,
        out_specs=[vmem] * 2,
        out_shape=[shape(24, LANES)] * 2,
        scratch_shapes=[
            buffer(COMPS, 2, 1, LANES),
            buffer(COMPS, 2, 1, LANES),
            buffer(2, 2, 1, LANES, dtype=ints),
            buffer(2, 2, 1, LANES, dtype=ints),
            buffer(2, COLS, dtype=ints),
            pltpu.SemaphoreType.DMA((5,)),
        ],
        compiler_params=params,
        name="pack_columns",
    )(*(pltpu.with_memory_space_constraint(x, pltpu.HBM) for x in (particles, contact_pairs, contact_count)))
    got_far = swapped(far, "span", 1)
    got_near = swapped(near, "span", 0)
    on_first, on_second, to_near, to_far, ext, infos, stays, landing = pl.pallas_call(
        inner_terms,
        in_specs=[vmem] * 6 + [smem],
        out_specs=[vmem] * 8,
        out_shape=[
            shape(16 * COLS, LANES),
            shape(16 * COLS, LANES),
            shape(PAYLOAD, LANES),
            shape(PAYLOAD, LANES),
            shape(COMPS, 2, EXT, LANES),
            shape(2, COLS, LANES),
            shape(2, COLS, LANES, dtype=ints),
            shape(16, LANES, dtype=ints),
        ],
        compiler_params=params,
        name="inner_terms",
    )(particles, contact_pairs, contact_count, filled, movers_out, movers_in, move_count)
    to_far, to_near, edges, edge_first, edge_second = pl.pallas_call(
        edge_terms,
        in_specs=[vmem] * 7,
        out_specs=[vmem] * 5,
        out_shape=[
            shape(PAYLOAD, LANES),
            shape(PAYLOAD, LANES),
            shape(96, LANES),
            shape(64, LANES),
            shape(64, LANES),
        ],
        compiler_params=params,
        name="edge_terms",
    )(got_near, got_far, near, far, infos, to_near, to_far)
    row_far = swapped(to_far, "blade", 1)
    row_near = swapped(to_near, "blade", 0)
    sums, ext, first_low, lists_low = pl.pallas_call(
        own_sums,
        in_specs=[vmem] * 9,
        out_specs=[vmem] * 4,
        out_shape=[
            shape(2, 7, COLS, LANES),
            shape(COMPS, 2, EXT, LANES),
            shape(COMPS, SLAB, LANES),
            shape(3, SLAB, LANES, dtype=ints),
        ],
        scratch_shapes=[buffer(34 * 40, LANES), buffer(34 * 16, LANES)],
        compiler_params=params,
        name="own_sums",
    )(particles, contact_pairs, contact_count, on_first, on_second, edges, edge_first, edge_second, ext)
    own = (sums, ext, first_low, lists_low, stays, landing)
    scratch = [
        buffer(COMPS, EXT, LANES),
        buffer(8 * SLAB, LANES),
        buffer(2, SLAB, LANES, dtype=ints),
        buffer(35 * 24, LANES),
    ]
    half = pl.pallas_call(
        far_row,
        in_specs=[vmem] * 7,
        out_specs=vmem,
        out_shape=shape(COMPS, COLS, LANES),
        scratch_shapes=scratch,
        compiler_params=params,
        name="far_row",
    )(row_far, *own)
    return pl.pallas_call(
        near_row,
        in_specs=[vmem] * 8,
        out_specs=vmem,
        out_shape=shape(COMPS, 2, COLS, LANES),
        scratch_shapes=scratch,
        compiler_params=params,
        name="near_row",
    )(row_near, half, *own)


def solution(mesh):
    return jax.shard_map(
        body,
        mesh=mesh,
        in_specs=(
            P(None, "blade", "span", None),
            P("blade", "span"),
            P(None, "blade", "span", None),
            P("blade", "span"),
            P(None, None, "blade", "span"),
            P(None, None, "blade", "span"),
            P(None, "blade", "span"),
        ),
        out_specs=P(None, "blade", "span", None),
        check_vma=False,
    )
```

```python
import jax
import jax.numpy as jnp
from jax import lax
from jax.experimental import pallas as pl
from jax.experimental.pallas import tpu as pltpu
from jax.sharding import PartitionSpec as P

spring = 4.0
normal_damp = 0.5
tangent_damp = 0.3
conduct = 40.0
timestep = 0.05
density = 100.0
gravity = 9.81
soft_len = 0.05

COMPS = 11
LANES = 128
LIVE = 96
COLS = 32
SLAB = 40
EXT = 56
BASE = 8
SOURCES = 34
EDGE = COMPS * COLS
PAYLOAD = EDGE + 24
row_steps = (0, 1, 0, 1, 1)
col_steps = (0, 0, 1, 1, -1)


def iota(shape, dim):
    return lax.broadcasted_iota(jnp.int32, shape, dim)


def pick(values, index):
    return jnp.take_along_axis(values, index, axis=1, mode="promise_in_bounds")


def to_column(row, size):
    n = row.shape[1]
    spread = jnp.where(iota((size, n), 0) == iota((size, n), 1), row, 0)
    return jnp.sum(spread, axis=1, keepdims=True)


def cross(a, b):
    return (
        a[1] * b[2] - a[2] * b[1],
        a[2] * b[0] - a[0] * b[2],
        a[0] * b[1] - a[1] * b[0],
    )


def pair_terms(first, second, row_shift, col_shift, listed):
    gap = (second[0] + row_shift - first[0], second[1] + col_shift - first[1], second[2] - first[2])
    dist = jnp.sqrt(gap[0] * gap[0] + gap[1] * gap[1] + gap[2] * gap[2] + soft_len * soft_len)
    inverse = 1.0 / dist
    n = tuple(g * inverse for g in gap)
    r1, r2 = first[9], second[9]
    intersection = r1 + r2 - dist
    spin = tuple(r1 * first[6 + i] + r2 * second[6 + i] for i in range(3))
    turn = cross(spin, n)
    w = tuple(second[3 + i] - first[3 + i] - turn[i] for i in range(3))
    u = w[0] * n[0] + w[1] * n[1] + w[2] * n[2]
    fric = tuple(tangent_damp * (w[i] - u * n[i]) for i in range(3))
    push = normal_damp * u - spring * intersection
    force = tuple(push * n[i] + fric[i] for i in range(3))
    torque = cross(n, fric)
    denom = jnp.where(listed, r1 + r2, 1.0)
    heat = 2.0 * conduct * r1 * r2 / denom * (second[10] - first[10])
    on_first = [*force, *(r1 * t for t in torque), heat]
    on_second = [*(-f for f in force), *(r2 * t for t in torque), -heat]
    return (
        [jnp.where(listed, t, 0.0) for t in on_first],
        [jnp.where(listed, t, 0.0) for t in on_second],
    )


def stepped(state, totals, live):
    r = state[9] + jnp.where(live, 0.0, 1.0)
    mass = density * r * r * r
    per_mass = timestep / mass
    per_inertia = timestep / (0.4 * mass * r * r)
    v = [state[3] + per_mass * totals[0], state[4] + per_mass * totals[1]]
    v.append(state[5] + per_mass * totals[2] - timestep * gravity)
    spin = [state[6 + i] + per_inertia * totals[3 + i] for i in range(3)]
    x = [state[i] + timestep * v[i] for i in range(3)]
    warmth = state[10] + per_mass * totals[6]
    return [jnp.where(live, t, 0.0) for t in [*x, *v, *spin, state[9], warmth]]


def shifts(heading):
    row_shift = jnp.where((heading == 0) | (heading == 2), 0.0, 1.0)
    col_shift = jnp.where(
        (heading == 2) | (heading == 3), 1.0, jnp.where(heading == 4, -1.0, 0.0)
    )
    return row_shift, col_shift


def keep(ref, base, terms):
    n = terms[0].shape[0]
    for j in range(7):
        ref[base + j * n : base + (j + 1) * n, :] = terms[j]
    ref[base + 7 * n : base + 8 * n, :] = jnp.zeros((n, LANES), jnp.float32)


def halves(x):
    high = x.astype(jnp.bfloat16).astype(jnp.float32)
    return jnp.concatenate([high, x - high], 0).astype(jnp.bfloat16)


def one_hot(index_row):
    hot = iota((LANES, LANES), 0) == index_row
    return jnp.where(hot, 1.0, 0.0).astype(jnp.bfloat16)


def spread(left, *index_rows):
    hot = jnp.concatenate([one_hot(row) for row in index_rows], 1)
    out = lax.dot_general(
        halves(left), hot, (((1,), (1,)), ((), ())), preferred_element_type=jnp.float32
    )
    rows = left.shape[0]
    return out[:rows] + out[rows:]


def packed(j, value, lists, count, info):
    lane = iota(value.shape, 1)
    if j < 8:
        extra = lists[j // 4].astype(jnp.float32)
        if j % 4 != 3:
            extra = pltpu.roll(extra, LIVE - 32 * (j % 4), 1)
    elif j == 8:
        extra = count.astype(jnp.float32)
    elif j == 9 and info is not None:
        extra = info
    else:
        return value
    return jnp.where(lane < LIVE, value, extra)


def unpacked(rows):
    lane = iota(rows[0].shape, 1)
    lists = []
    for half in range(2):
        value = rows[half * 4 + 3]
        for k in range(3):
            moved = pltpu.roll(rows[half * 4 + k], 32 * k + 32, 1)
            value = jnp.where(lane // 32 == k, moved, value)
        lists.append(value.astype(jnp.int32))
    return lists


def lane_of(value, k):
    return value[:, LIVE + k : LIVE + k + 1]


def pack_columns(particles, pairs, count, far, near, p_west, p_east, c_west, c_east, n_all, sems):
    last = COLS - 1
    copies = [
        pltpu.make_async_copy(particles.at[:, :, 0:1, :], p_west, sems.at[0]),
        pltpu.make_async_copy(particles.at[:, :, last:COLS, :], p_east, sems.at[1]),
        pltpu.make_async_copy(pairs.at[:, :, 0:1, :], c_west, sems.at[2]),
        pltpu.make_async_copy(pairs.at[:, :, last:COLS, :], c_east, sems.at[3]),
        pltpu.make_async_copy(count, n_all, sems.at[4]),
    ]
    for copy in copies:
        copy.start()
    near[...] = jnp.zeros(near.shape, jnp.float32)
    far[...] = jnp.zeros(far.shape, jnp.float32)
    odd = lax.rem(lax.axis_index("span"), 2) == 1
    for copy in copies:
        copy.wait()
    for r in range(2):
        n_row = n_all[r : r + 1, :]
        sides = []
        for p, c, at, cell in ((p_west, c_west, 0, 0), (p_east, c_east, 0, COLS - 1)):
            n = jnp.sum(jnp.where(iota((1, COLS), 1) == cell, n_row, 0), axis=1, keepdims=True)
            lists = [c[k, r, at : at + 1, :] for k in range(2)]
            sides.append([packed(j, p[j, r, at : at + 1, :], lists, n, None) for j in range(COMPS)])
        for j in range(COMPS):
            west, east = sides[0][j], sides[1][j]
            row = r * 12 + j
            near[row : row + 1, :] = jnp.where(odd, west, east)
            far[row : row + 1, :] = jnp.where(odd, east, west)


def leavers(movers, counts, row):
    direction = 1 - row
    cells = lax.rem(movers[direction, 0], COLS)
    slots = movers[direction, 1]
    n = cells.shape[1]
    number = iota((COLS, n), 1)
    here = (iota((COLS, n), 0) == cells) & (number < counts[direction, 0, 0])
    slot = jnp.sum(jnp.where(here, slots + 1, 0), axis=1, keepdims=True)
    which = jnp.sum(jnp.where(here, number, 0), axis=1, keepdims=True)
    return slot, which


def roll_cells(value, step):
    return pltpu.roll(value, step % value.shape[0], 0)


def inner_terms(
    particles, pairs, count, filled, movers, arrivals, counts,
    on_first, on_second, to_near, to_far, ext, infos, stays, landing,
):
    lane = iota((COLS, LANES), 1)
    column = iota((COLS, LANES), 0)
    zeros = jnp.zeros((8, LANES), jnp.float32)
    for r in range(2):
        for j in range(COMPS):
            ext[j, r, 0:8, :] = zeros
            ext[j, r, 40:48, :] = zeros
            ext[j, r, 8:40, :] = particles[j, r]
    counted = [to_column(count[r : r + 1, :], COLS) for r in range(2)]
    hits = []
    for r in range(2):
        headings = (0, 1, 2, 3, 4) if r == 0 else (0, 2)
        first_index = pairs[0, r]
        heading = pairs[1, r] // LANES
        target = lax.rem(pairs[1, r], LANES)
        outside = (column == COLS - 1) & ((heading == 2) | (heading == 3)) | (column == 0) & (heading == 4)
        listed = (lane < counted[r]) & ~outside
        if r == 1:
            listed = listed & ((heading == 0) | (heading == 2))
        row_shift, col_shift = shifts(heading)
        for g in range(0, COLS, 8):
            rows = slice(g, g + 8)
            first = [pick(particles[j, r, rows, :], first_index[rows]) for j in range(COMPS)]
            second = []
            for j in range(COMPS):
                value = None
                for d in headings:
                    at = BASE + col_steps[d] + g
                    got = pick(ext[j, r + row_steps[d], at : at + 8, :], target[rows])
                    value = got if value is None else jnp.where(heading[rows] == d, got, value)
                second.append(value)
            f, s = pair_terms(first, second, row_shift[rows], col_shift[rows], listed[rows])
            for ref, terms in ((on_first, f), (on_second, s)):
                for j in range(7):
                    at = (r * 8 + j) * COLS + g
                    ref[at : at + 8, :] = terms[j]
        for ref in (on_first, on_second):
            at = (r * 8 + 7) * COLS
            ref[at : at + COLS, :] = jnp.zeros((COLS, LANES), jnp.float32)
        hits.append((first_index, heading, target))

    for r in range(2):
        slot, which = leavers(movers, counts, r)
        live = lane < to_column(filled[r : r + 1, :], COLS)
        stays[r] = jnp.where(live, jnp.where(lane != slot - 1, 2, 1), 0)
        cells = to_column(lax.rem(arrivals[r, 0], COLS), 16)
        slots = to_column(arrivals[r, 1], 16)
        hit = slots == iota((16, LANES), 1)
        number = jnp.sum(jnp.where(hit, iota((16, LANES), 0) + 1, 0), axis=0, keepdims=True) - 1
        cell = jnp.sum(jnp.where(hit, cells, 0), axis=0, keepdims=True)
        landing[8 * r : 8 * r + 1, :] = number
        landing[8 * r + 1 : 8 * r + 2, :] = jnp.where(number >= 0, cell, -1)
        wide = jnp.broadcast_to(slot - 1, (COLS, LANES))
        first_index, heading, target = hits[r]
        own_first = first_index == wide
        own_second = (heading == 0) & (target == wide)
        from_left = (heading == 2) & (target == roll_cells(wide, -1))
        if r == 1:
            _, above, aim = hits[0]
            straight = (above == 1) & (aim == wide)
            slant = (above == 3) & (aim == roll_cells(wide, -1))
            back = (above == 4) & (aim == roll_cells(wide, 1))
        info = jnp.where(lane == LIVE + 7, slot.astype(jnp.float32), which.astype(jnp.float32))
        for j in range(7):
            base = (r * 8 + j) * COLS
            f = on_first[base : base + COLS, :]
            s = on_second[base : base + COLS, :]
            total = jnp.where(own_first, f, 0.0) + jnp.where(own_second, s, 0.0)
            right = jnp.where(from_left, s, 0.0)
            if r == 1:
                u = on_second[j * COLS : (j + 1) * COLS, :]
                total = total + jnp.where(straight, u, 0.0)
                right = right + jnp.where(slant, u, 0.0)
                total = total + roll_cells(jnp.where(back, u, 0.0), -1)
            total = total + roll_cells(right, 1)
            info = jnp.where(lane == LIVE + j, jnp.sum(total, axis=1, keepdims=True), info)
        infos[r] = info

    turn = lax.rem(lax.axis_index("blade"), 2)
    for out, row in ((to_near, 1 - turn), (to_far, turn)):
        n = jnp.where(row == 1, counted[1], counted[0])
        lists = [pairs[k, row] for k in range(2)]
        for j in range(COMPS):
            value = packed(j, particles[j, row], lists, jnp.broadcast_to(n, (COLS, LANES)), infos[row])
            out[j * COLS : (j + 1) * COLS, :] = value


def edge_terms(
    got_near, got_far, sent_near, sent_far, infos, near_in, far_in, to_far, to_near, edges, edge_first, edge_second
):
    to_near[0:EDGE, :] = near_in[0:EDGE, :]
    to_far[0:EDGE, :] = far_in[0:EDGE, :]
    odd = lax.rem(lax.axis_index("span"), 2) == 1
    west = jnp.where(odd, got_near[...], got_far[...])
    east = jnp.where(odd, got_far[...], got_near[...])
    west_own = jnp.where(odd, sent_near[...], sent_far[...])
    east_own = jnp.where(odd, sent_far[...], sent_near[...])
    for k, side in enumerate((west, west_own, east_own, east)):
        for r in range(2):
            edges[pl.ds(4 * r + k, 12, stride=8), :] = side[r * 12 : r * 12 + 12]
    tile = [edges[j * 8 : j * 8 + 8, :] for j in range(COMPS)]
    first_index, second_index = unpacked(tile[:8])
    heading = second_index // LANES
    target = lax.rem(second_index, LANES)
    spot = iota((8, LANES), 0)
    lane = iota((8, LANES), 1)
    even = lax.rem(spot, 2) == 0
    listed = lane < lane_of(tile[8], 0).astype(jnp.int32)
    listed = listed & (
        ((heading == 2) & even)
        | ((heading == 3) & even & (spot < 4))
        | ((heading == 4) & ~even & (spot < 4))
    )
    first = [pick(t, first_index) for t in tile]
    second = []
    for t in tile:
        beside = pick(roll_cells(t, -1), target)
        below = pick(jnp.where(even, roll_cells(t, -5), roll_cells(t, -3)), target)
        second.append(jnp.where(heading == 2, beside, below))
    row_shift, col_shift = shifts(heading)
    f, s = pair_terms(first, second, row_shift, col_shift, listed)
    keep(edge_first, 0, f)
    keep(edge_second, 0, s)

    slots = [[lane_of(infos[r, c : c + 1, :], 7).astype(jnp.int32) for c in (0, COLS - 1)] for r in range(2)]

    def at_spots(*choices):
        value = jnp.zeros((8, LANES), jnp.int32)
        for k, slot in choices:
            value = jnp.where(spot == k, slot, value)
        return value - 1

    mine = first_index == at_spots((1, slots[0][0]), (2, slots[0][1]), (6, slots[1][1]))
    beside = (heading == 2) & (target == at_spots((0, slots[0][0]), (4, slots[1][0])))
    below = (heading != 2) & (target == at_spots((0, slots[1][0]), (3, slots[1][1])))
    sums = [jnp.zeros((8, LANES), jnp.float32)] * 3
    for j in range(7):
        for k, (hit, term) in enumerate(((mine, f[j]), (beside, s[j]), (below, s[j]))):
            total = jnp.sum(jnp.where(hit, term, 0.0), axis=1, keepdims=True)
            sums[k] = jnp.where(lane == LIVE + j, total, sums[k])
    fixes = (
        (sums[0][1:2] + sums[1][0:1], sums[0][2:3]),
        (sums[1][4:5] + sums[2][0:1], sums[0][6:7] + sums[2][3:4]),
    )
    turn = lax.rem(lax.axis_index("blade"), 2)
    for out, row in ((to_near, 1 - turn), (to_far, turn)):
        low = row == 1
        for k, c in enumerate((0, COLS - 1)):
            at = 9 * COLS + c
            out[at : at + 1, :] += jnp.where(low, fixes[1][k], fixes[0][k])
        out[EDGE : EDGE + 12, :] = jnp.where(low, east[12:24], east[0:12])
        out[EDGE + 12 : EDGE + 24, :] = jnp.where(low, west[12:24], west[0:12])


def own_sums(
    particles, pairs, count, on_first, on_second, edges, edge_first, edge_second,
    ext_in, sums, ext, first_low, lists_low, by_source0, by_source1,
):
    ext[...] = ext_in[...]
    sizes = (40, 16)
    for ref, size in ((by_source0, 40), (by_source1, 16)):
        ref[0:size, :] = jnp.zeros((size, LANES), jnp.float32)
        ref[33 * size : 34 * size, :] = jnp.zeros((size, LANES), jnp.float32)
    blank = jnp.zeros((8, LANES), jnp.float32)
    for r, (ref, headings) in enumerate(((by_source0, (0, 1, 2, 3, 4)), (by_source1, (0, 2)))):

        def source(c, _, r=r, ref=ref, headings=headings):
            f = on_first[pl.ds(r * 8 * COLS + c, 8, stride=COLS), :]
            s = on_second[pl.ds(r * 8 * COLS + c, 8, stride=COLS), :]
            second_row = pairs[1, r, pl.ds(c, 1), :]
            heading = second_row // LANES
            left = jnp.concatenate(
                [jnp.concatenate([f if d == 0 else blank, jnp.where(heading == d, s, 0.0)], 1) for d in headings],
                0,
            )
            out = spread(left, pairs[0, r, pl.ds(c, 1), :], lax.rem(second_row, LANES))
            size = sizes[r]
            ref[pl.ds(pl.multiple_of((c + 1) * size, 8), size), :] = out
            return 0

        lax.fori_loop(0, COLS, source, 0, unroll=32)
    tile = [edges[j * 8 : j * 8 + 8, :] for j in range(COMPS)]
    first_index, second_index = unpacked(tile[:8])
    heading = second_index // LANES
    target = lax.rem(second_index, LANES)
    for k in (0, 1, 2, 3, 4, 6):
        f = edge_first[pl.ds(k, 8, stride=8), :]
        s = edge_second[pl.ds(k, 8, stride=8), :]
        aim = heading[k : k + 1]
        left = jnp.concatenate(
            [
                jnp.concatenate([f, blank], 1),
                jnp.concatenate([blank, jnp.where(aim == 2, s, 0.0)], 1),
                jnp.concatenate([blank, jnp.where(aim == 2, 0.0, s)], 1),
                jnp.zeros((8, 2 * LANES), jnp.float32),
            ],
            0,
        )
        out = spread(left, first_index[k : k + 1], target[k : k + 1])
        if k == 0:
            by_source0[16:24, :] = out[8:16]
            by_source0[24:32, :] = out[16:24]
        elif k == 1:
            by_source0[40:48, :] += out[0:8]
        elif k == 2:
            by_source0[32 * 40 : 32 * 40 + 8, :] += out[0:8]
        elif k == 3:
            by_source0[33 * 40 + 32 : 33 * 40 + 40, :] = out[16:24]
        elif k == 4:
            by_source1[8:16, :] = out[8:16]
        else:
            by_source1[32 * 16 : 32 * 16 + 8, :] += out[0:8]

    def column(ref, size, tile_at, shift, j):
        return ref[pl.ds((1 + shift) * size + tile_at * 8 + j, COLS, stride=size), :]

    for j in range(7):
        sums[0, j] = column(by_source0, 40, 0, 0, j) + column(by_source0, 40, 2, -1, j)
        total = column(by_source1, 16, 0, 0, j) + column(by_source1, 16, 1, -1, j)
        total = total + column(by_source0, 40, 1, 0, j) + column(by_source0, 40, 3, -1, j)
        sums[1, j] = total + column(by_source0, 40, 4, 1, j)

    for r in range(2):
        for j in range(COMPS):
            for k, at in ((3, 40), (0, 41), (1, 42), (0, 7)):
                ext[j, r, at : at + 1, :] = tile[j][4 * r + k : 4 * r + k + 1]
    rows = jnp.concatenate([pairs[0, 1], first_index[7:8], first_index[4:5], jnp.zeros((6, LANES), jnp.int32)], 0)
    seconds = jnp.concatenate([pairs[1, 1], second_index[7:8], second_index[4:5], jnp.zeros((6, LANES), jnp.int32)], 0)
    edge_count = lane_of(tile[8], 0).astype(jnp.int32)
    n = jnp.concatenate(
        [to_column(count[1:2, :], COLS), edge_count[7:8], edge_count[4:5], jnp.zeros((6, 1), jnp.int32)], 0
    )
    lists_low[0] = rows
    lists_low[1] = jnp.where(iota((SLAB, LANES), 1) < n, seconds // LANES, -1)
    lists_low[2] = lax.rem(seconds, LANES)
    for j in range(COMPS):
        first_low[j] = pick(ext[j, 1, BASE : BASE + SLAB, :], rows)


def surround(around, source):
    zeros = jnp.zeros((8, LANES), jnp.float32)
    for j in range(COMPS):
        main = source[j * COLS : (j + 1) * COLS, :]
        right = source[EDGE + j : EDGE + j + 1, :]
        left = source[EDGE + 12 + j : EDGE + 13 + j, :]
        around[j, 40:48, :] = zeros
        around[j, 8:40, :] = main
        around[j, 40:41, :] = right
        around[j, 41:42, :] = left
        around[j, 42:43, :] = main[0:1]
        around[j, 7:8, :] = left


def row_terms(first, others, heading, target):
    _, col_shift = shifts(heading)
    pieces = []
    for g in range(0, SLAB, 8):
        rows = slice(g, g + 8)
        aim = heading[rows]
        second = []
        for j in range(COMPS):
            value = None
            for d in (1, 3, 4):
                got = pick(others(j, BASE + col_steps[d] + g), target[rows])
                value = got if value is None else jnp.where(aim == d, got, value)
            second.append(value)
        listed = (aim == 1) | (aim == 3) | (aim == 4)
        pieces.append(pair_terms([first(j, rows) for j in range(COMPS)], second, 1.0, col_shift[rows], listed))
    return [[jnp.concatenate([piece[k][j] for piece in pieces], 0) for j in range(7)] for k in range(2)]


def finish(side, info, state, leaving, totals, ext, stays, landing, write):
    slot = lane_of(info, 7).astype(jnp.int32)
    which = lane_of(info, 8).astype(jnp.int32)
    leaves = slot > 0
    leaving = [t + lane_of(info, j) for j, t in enumerate(leaving)]
    at_slot = jnp.broadcast_to(jnp.maximum(slot - 1, 0), (COLS, LANES))
    moved = stepped([pick(v, at_slot) for v in state], leaving, leaves)
    moved[0] = moved[0] + (-1.0 if side == 0 else 1.0)
    match = (which == landing[8 * side : 8 * side + 1, :]) & leaves
    rows = stepped([ext[j, side, BASE : BASE + COLS, :] for j in range(COMPS)], totals, stays[side] > 0)
    lands = iota((COLS, LANES), 0) == landing[8 * side + 1 : 8 * side + 2, :]
    for j in range(COMPS):
        value = jnp.sum(jnp.where(match, moved[j], 0.0), axis=0, keepdims=True)
        write(side, j, jnp.where(lands, value, jnp.where(stays[side] == 1, 0.0, rows[j])))


def from_behind(source, sums, ext, stays, landing, write, around, terms, indices, by_source):
    surround(around, source)
    lane = iota((SLAB, LANES), 1)
    rows = [around[j, BASE : BASE + SLAB, :] for j in range(COMPS)]
    firsts, seconds = unpacked(rows[:8])
    heading = jnp.where(lane < lane_of(rows[8], 0).astype(jnp.int32), seconds // LANES, -1)
    target = lax.rem(seconds, LANES)
    f, s = row_terms(
        lambda j, at: pick(rows[j][at], firsts[at]), lambda j, at: ext[j, 0, at : at + 8, :], heading, target
    )
    keep(terms, 0, s)
    indices[0] = heading
    indices[1] = target
    for c in range(SOURCES):
        term = terms[pl.ds(c, 8, stride=SLAB), :]
        aim = indices[0, c : c + 1, :]
        left = jnp.concatenate([jnp.where(aim == d, term, 0.0) for d in (1, 3, 4)], 0)
        by_source[(c + 1) * 24 : (c + 2) * 24, :] = spread(left, indices[1, c : c + 1, :])
    by_source[0:24, :] = by_source[34 * 24 : 35 * 24, :]
    info = rows[9][:COLS]
    hit = firsts[:COLS] == lane_of(info, 7).astype(jnp.int32) - 1
    leaving = [jnp.sum(jnp.where(hit, f[j][:COLS], 0.0), axis=1, keepdims=True) for j in range(7)]
    totals = []
    for j in range(7):
        total = sums[0, j]
        for k, shift in ((0, 0), (1, -1), (2, 1)):
            total = total + by_source[pl.ds((1 + shift) * 24 + k * 8 + j, COLS, stride=24), :]
        totals.append(total)
    state = [v[:COLS] for v in rows]
    finish(0, info, state, leaving, totals, ext, stays, landing, write)


def from_ahead(source, sums, ext, first_low, lists_low, stays, landing, write, around, terms, by_source):
    surround(around, source)
    heading, target = lists_low[1], lists_low[2]
    f, s = row_terms(
        lambda j, at: first_low[j, at, :], lambda j, at: around[j, at : at + 8, :], heading, target
    )
    keep(terms, 0, f)
    for c in range(COLS):
        by_source[c * 8 : c * 8 + 8, :] = spread(terms[pl.ds(c, 8, stride=SLAB), :], lists_low[0, c : c + 1, :])
    info = around[9, BASE : BASE + COLS, :]
    wide = jnp.broadcast_to(lane_of(info, 7).astype(jnp.int32) - 1, (COLS, LANES))
    wide = jnp.concatenate([wide, jnp.full((8, LANES), -1, jnp.int32)], 0)
    up = jnp.where(iota((SLAB, LANES), 0) == 33, wide[0:1], roll_cells(wide, -1))
    straight = (heading == 1) & (target == wide)
    slanting = (heading == 3) & (target == up)
    back = (heading == 4) & (target == roll_cells(wide, 1))
    first_cell = iota((COLS, LANES), 0) == 0
    leaving = []
    for j in range(7):
        slant = jnp.where(slanting, s[j], 0.0)
        slant = jnp.where(first_cell, slant[33:34], roll_cells(slant, 1)[:COLS])
        total = jnp.where(straight, s[j], 0.0)[:COLS] + slant
        total = total + roll_cells(jnp.where(back, s[j], 0.0), -1)[:COLS]
        leaving.append(jnp.sum(total, axis=1, keepdims=True))
    totals = [sums[1, j] + by_source[pl.ds(j, COLS, stride=8), :] for j in range(7)]
    state = [around[j, BASE : BASE + COLS, :] for j in range(COMPS)]
    finish(1, info, state, leaving, totals, ext, stays, landing, write)


def far_row(far, sums, ext, first_low, lists_low, stays, landing, half, around, terms, indices, by_source):
    odd = lax.rem(lax.axis_index("blade"), 2) == 1

    def write(side, j, value):
        half[j] = value

    @pl.when(odd)
    def _():
        from_ahead(far, sums, ext, first_low, lists_low, stays, landing, write, around, terms, by_source)

    @pl.when(jnp.logical_not(odd))
    def _():
        from_behind(far, sums, ext, stays, landing, write, around, terms, indices, by_source)


def near_row(near, half, sums, ext, first_low, lists_low, stays, landing, out, around, terms, indices, by_source):
    odd = lax.rem(lax.axis_index("blade"), 2) == 1

    def write(side, j, value):
        out[j, side] = value
        out[j, 1 - side] = half[j]

    @pl.when(odd)
    def _():
        from_behind(near, sums, ext, stays, landing, write, around, terms, indices, by_source)

    @pl.when(jnp.logical_not(odd))
    def _():
        from_ahead(near, sums, ext, first_low, lists_low, stays, landing, write, around, terms, by_source)


def swapped(block, axis, start):
    pairs = []
    for i in range(start, lax.axis_size(axis) - 1, 2):
        pairs += [(i, i + 1), (i + 1, i)]
    return lax.ppermute(block, axis, pairs)


vmem = pl.BlockSpec(memory_space=pltpu.VMEM)
smem = pl.BlockSpec(memory_space=pltpu.SMEM)
hbm = pl.BlockSpec(memory_space=pltpu.HBM)
params = pltpu.CompilerParams(vmem_limit_bytes=24 * 1024 * 1024)


def shape(*dims, dtype=jnp.float32):
    return jax.ShapeDtypeStruct(dims, dtype)


def buffer(*dims, dtype=jnp.float32):
    return pltpu.VMEM(dims, dtype)


def body(particles, filled, contact_pairs, contact_count, movers_out, movers_in, move_count):
    ints = jnp.int32
    far, near = pl.pallas_call(
        pack_columns,
        in_specs=[hbm] * 3,
        out_specs=[vmem] * 2,
        out_shape=[shape(24, LANES)] * 2,
        scratch_shapes=[
            buffer(COMPS, 2, 1, LANES),
            buffer(COMPS, 2, 1, LANES),
            buffer(2, 2, 1, LANES, dtype=ints),
            buffer(2, 2, 1, LANES, dtype=ints),
            buffer(2, COLS, dtype=ints),
            pltpu.SemaphoreType.DMA((5,)),
        ],
        compiler_params=params,
        name="pack_columns",
    )(*(pltpu.with_memory_space_constraint(x, pltpu.HBM) for x in (particles, contact_pairs, contact_count)))
    got_far = swapped(far, "span", 1)
    got_near = swapped(near, "span", 0)
    on_first, on_second, to_near, to_far, ext, infos, stays, landing = pl.pallas_call(
        inner_terms,
        in_specs=[vmem] * 6 + [smem],
        out_specs=[vmem] * 8,
        out_shape=[
            shape(17 * COLS, LANES),
            shape(17 * COLS, LANES),
            shape(PAYLOAD, LANES),
            shape(PAYLOAD, LANES),
            shape(COMPS, 2, EXT, LANES),
            shape(2, COLS, LANES),
            shape(2, COLS, LANES, dtype=ints),
            shape(16, LANES, dtype=ints),
        ],
        compiler_params=params,
        name="inner_terms",
    )(particles, contact_pairs, contact_count, filled, movers_out, movers_in, move_count)
    to_far, to_near, edges, edge_first, edge_second = pl.pallas_call(
        edge_terms,
        in_specs=[vmem] * 7,
        out_specs=[vmem] * 5,
        out_shape=[
            shape(PAYLOAD, LANES),
            shape(PAYLOAD, LANES),
            shape(104, LANES),
            shape(72, LANES),
            shape(72, LANES),
        ],
        compiler_params=params,
        name="edge_terms",
    )(got_near, got_far, near, far, infos, to_near, to_far)
    row_far = swapped(to_far, "blade", 1)
    row_near = swapped(to_near, "blade", 0)
    sums, ext, first_low, lists_low = pl.pallas_call(
        own_sums,
        in_specs=[vmem] * 9,
        out_specs=[vmem] * 4,
        out_shape=[
            shape(2, 7, COLS, LANES),
            shape(COMPS, 2, EXT, LANES),
            shape(COMPS, SLAB, LANES),
            shape(3, SLAB, LANES, dtype=ints),
        ],
        scratch_shapes=[buffer(35 * 40, LANES), buffer(34 * 16, LANES)],
        compiler_params=params,
        name="own_sums",
    )(particles, contact_pairs, contact_count, on_first, on_second, edges, edge_first, edge_second, ext)
    own = (sums, ext, first_low, lists_low, stays, landing)
    scratch = [
        buffer(COMPS, EXT, LANES),
        buffer(9 * SLAB, LANES),
        buffer(2, SLAB, LANES, dtype=ints),
        buffer(35 * 24, LANES),
    ]
    half = pl.pallas_call(
        far_row,
        in_specs=[vmem] * 7,
        out_specs=vmem,
        out_shape=shape(COMPS, COLS, LANES),
        scratch_shapes=scratch,
        compiler_params=params,
        name="far_row",
    )(row_far, *own)
    return pl.pallas_call(
        near_row,
        in_specs=[vmem] * 8,
        out_specs=vmem,
        out_shape=shape(COMPS, 2, COLS, LANES),
        scratch_shapes=scratch,
        compiler_params=params,
        name="near_row",
    )(row_near, half, *own)


def solution(mesh):
    return jax.shard_map(
        body,
        mesh=mesh,
        in_specs=(
            P(None, "blade", "span", None),
            P("blade", "span"),
            P(None, "blade", "span", None),
            P("blade", "span"),
            P(None, None, "blade", "span"),
            P(None, None, "blade", "span"),
            P(None, "blade", "span"),
        ),
        out_specs=P(None, "blade", "span", None),
        check_vma=False,
    )
```

```python
import jax
import jax.numpy as jnp
from jax import lax
from jax.experimental import pallas as pl
from jax.experimental.pallas import tpu as pltpu
from jax.sharding import PartitionSpec as P

spring = 4.0
normal_damp = 0.5
tangent_damp = 0.3
conduct = 40.0
timestep = 0.05
density = 100.0
gravity = 9.81
soft_len = 0.05

COMPS = 11
LANES = 128
LIVE = 96
COLS = 32
SLAB = 40
EXT = 56
BASE = 8
SOURCES = 34
EDGE = COMPS * COLS
PAYLOAD = EDGE + 24
row_steps = (0, 1, 0, 1, 1)
col_steps = (0, 0, 1, 1, -1)


def iota(shape, dim):
    return lax.broadcasted_iota(jnp.int32, shape, dim)


def pick(values, index):
    return jnp.take_along_axis(values, index, axis=1, mode="promise_in_bounds")


def to_column(row, size):
    n = row.shape[1]
    spread = jnp.where(iota((size, n), 0) == iota((size, n), 1), row, 0)
    return jnp.sum(spread, axis=1, keepdims=True)


def cross(a, b):
    return (
        a[1] * b[2] - a[2] * b[1],
        a[2] * b[0] - a[0] * b[2],
        a[0] * b[1] - a[1] * b[0],
    )


def pair_terms(first, second, row_shift, col_shift, listed):
    gap = (second[0] + row_shift - first[0], second[1] + col_shift - first[1], second[2] - first[2])
    dist = jnp.sqrt(gap[0] * gap[0] + gap[1] * gap[1] + gap[2] * gap[2] + soft_len * soft_len)
    inverse = 1.0 / dist
    n = tuple(g * inverse for g in gap)
    r1, r2 = first[9], second[9]
    intersection = r1 + r2 - dist
    spin = tuple(r1 * first[6 + i] + r2 * second[6 + i] for i in range(3))
    turn = cross(spin, n)
    w = tuple(second[3 + i] - first[3 + i] - turn[i] for i in range(3))
    u = w[0] * n[0] + w[1] * n[1] + w[2] * n[2]
    fric = tuple(tangent_damp * (w[i] - u * n[i]) for i in range(3))
    push = normal_damp * u - spring * intersection
    force = tuple(push * n[i] + fric[i] for i in range(3))
    torque = cross(n, fric)
    denom = jnp.where(listed, r1 + r2, 1.0)
    heat = 2.0 * conduct * r1 * r2 / denom * (second[10] - first[10])
    on_first = [*force, *(r1 * t for t in torque), heat]
    on_second = [*(-f for f in force), *(r2 * t for t in torque), -heat]
    return (
        [jnp.where(listed, t, 0.0) for t in on_first],
        [jnp.where(listed, t, 0.0) for t in on_second],
    )


def stepped(state, totals, live):
    r = state[9] + jnp.where(live, 0.0, 1.0)
    mass = density * r * r * r
    per_mass = timestep / mass
    per_inertia = timestep / (0.4 * mass * r * r)
    v = [state[3] + per_mass * totals[0], state[4] + per_mass * totals[1]]
    v.append(state[5] + per_mass * totals[2] - timestep * gravity)
    spin = [state[6 + i] + per_inertia * totals[3 + i] for i in range(3)]
    x = [state[i] + timestep * v[i] for i in range(3)]
    warmth = state[10] + per_mass * totals[6]
    return [jnp.where(live, t, 0.0) for t in [*x, *v, *spin, state[9], warmth]]


def shifts(heading):
    row_shift = jnp.where((heading == 0) | (heading == 2), 0.0, 1.0)
    col_shift = jnp.where(
        (heading == 2) | (heading == 3), 1.0, jnp.where(heading == 4, -1.0, 0.0)
    )
    return row_shift, col_shift


def keep(ref, base, terms):
    n = terms[0].shape[0]
    for j in range(7):
        ref[base + j * n : base + (j + 1) * n, :] = terms[j]
    ref[base + 7 * n : base + 8 * n, :] = jnp.zeros((n, LANES), jnp.float32)


def halves(x):
    high = x.astype(jnp.bfloat16).astype(jnp.float32)
    return jnp.concatenate([high, x - high], 0).astype(jnp.bfloat16)


def one_hot(index_row):
    hot = iota((LANES, LANES), 0) == index_row
    return jnp.where(hot, 1.0, 0.0).astype(jnp.bfloat16)


def spread(left, *index_rows):
    return gather_sums(left, jnp.concatenate([one_hot(row) for row in index_rows], 1))


def gather_sums(left, hot):
    out = lax.dot_general(
        halves(left), hot, (((1,), (1,)), ((), ())), preferred_element_type=jnp.float32
    )
    rows = left.shape[0]
    return out[:rows] + out[rows:]


def packed(j, value, lists, count, info):
    lane = iota(value.shape, 1)
    if j < 8:
        extra = lists[j // 4].astype(jnp.float32)
        if j % 4 != 3:
            extra = pltpu.roll(extra, LIVE - 32 * (j % 4), 1)
    elif j == 8:
        extra = count.astype(jnp.float32)
    elif j == 9 and info is not None:
        extra = info
    else:
        return value
    return jnp.where(lane < LIVE, value, extra)


def unpacked(rows):
    lane = iota(rows[0].shape, 1)
    lists = []
    for half in range(2):
        value = rows[half * 4 + 3]
        for k in range(3):
            moved = pltpu.roll(rows[half * 4 + k], 32 * k + 32, 1)
            value = jnp.where(lane // 32 == k, moved, value)
        lists.append(value.astype(jnp.int32))
    return lists


def lane_of(value, k):
    return value[:, LIVE + k : LIVE + k + 1]


def pack_columns(particles, pairs, count, far, near, p_west, p_east, c_west, c_east, n_all, sems):
    last = COLS - 1
    copies = [
        pltpu.make_async_copy(particles.at[:, :, 0:1, :], p_west, sems.at[0]),
        pltpu.make_async_copy(particles.at[:, :, last:COLS, :], p_east, sems.at[1]),
        pltpu.make_async_copy(pairs.at[:, :, 0:1, :], c_west, sems.at[2]),
        pltpu.make_async_copy(pairs.at[:, :, last:COLS, :], c_east, sems.at[3]),
        pltpu.make_async_copy(count, n_all, sems.at[4]),
    ]
    for copy in copies:
        copy.start()
    near[...] = jnp.zeros(near.shape, jnp.float32)
    far[...] = jnp.zeros(far.shape, jnp.float32)
    odd = lax.rem(lax.axis_index("span"), 2) == 1
    for copy in copies:
        copy.wait()
    for r in range(2):
        n_row = n_all[r : r + 1, :]
        sides = []
        for p, c, at, cell in ((p_west, c_west, 0, 0), (p_east, c_east, 0, COLS - 1)):
            n = jnp.sum(jnp.where(iota((1, COLS), 1) == cell, n_row, 0), axis=1, keepdims=True)
            lists = [c[k, r, at : at + 1, :] for k in range(2)]
            sides.append([packed(j, p[j, r, at : at + 1, :], lists, n, None) for j in range(COMPS)])
        for j in range(COMPS):
            west, east = sides[0][j], sides[1][j]
            row = r * 12 + j
            near[row : row + 1, :] = jnp.where(odd, west, east)
            far[row : row + 1, :] = jnp.where(odd, east, west)


def leavers(movers, counts, row):
    direction = 1 - row
    cells = lax.rem(movers[direction, 0], COLS)
    slots = movers[direction, 1]
    n = cells.shape[1]
    number = iota((COLS, n), 1)
    here = (iota((COLS, n), 0) == cells) & (number < counts[direction, 0, 0])
    slot = jnp.sum(jnp.where(here, slots + 1, 0), axis=1, keepdims=True)
    which = jnp.sum(jnp.where(here, number, 0), axis=1, keepdims=True)
    return slot, which


def roll_cells(value, step):
    return pltpu.roll(value, step % value.shape[0], 0)


def inner_terms(
    particles, pairs, count, filled, movers, arrivals, counts,
    on_first, on_second, to_near, to_far, ext, infos, stays, landing,
):
    lane = iota((COLS, LANES), 1)
    column = iota((COLS, LANES), 0)
    zeros = jnp.zeros((8, LANES), jnp.float32)
    for r in range(2):
        for j in range(COMPS):
            ext[j, r, 0:8, :] = zeros
            ext[j, r, 40:48, :] = zeros
            ext[j, r, 8:40, :] = particles[j, r]
    counted = [to_column(count[r : r + 1, :], COLS) for r in range(2)]
    hits = []
    for r in range(2):
        headings = (0, 1, 2, 3, 4) if r == 0 else (0, 2)
        first_index = pairs[0, r]
        heading = pairs[1, r] // LANES
        target = lax.rem(pairs[1, r], LANES)
        outside = (column == COLS - 1) & ((heading == 2) | (heading == 3)) | (column == 0) & (heading == 4)
        listed = (lane < counted[r]) & ~outside
        if r == 1:
            listed = listed & ((heading == 0) | (heading == 2))
        row_shift, col_shift = shifts(heading)
        for g in range(0, COLS, 8):
            rows = slice(g, g + 8)
            first = [pick(particles[j, r, rows, :], first_index[rows]) for j in range(COMPS)]
            second = []
            for j in range(COMPS):
                value = None
                for d in headings:
                    at = BASE + col_steps[d] + g
                    got = pick(ext[j, r + row_steps[d], at : at + 8, :], target[rows])
                    value = got if value is None else jnp.where(heading[rows] == d, got, value)
                second.append(value)
            f, s = pair_terms(first, second, row_shift[rows], col_shift[rows], listed[rows])
            for ref, terms in ((on_first, f), (on_second, s)):
                for j in range(7):
                    at = (r * 8 + j) * COLS + g
                    ref[at : at + 8, :] = terms[j]
        for ref in (on_first, on_second):
            at = (r * 8 + 7) * COLS
            ref[at : at + COLS, :] = jnp.zeros((COLS, LANES), jnp.float32)
        hits.append((first_index, heading, target))

    for r in range(2):
        slot, which = leavers(movers, counts, r)
        live = lane < to_column(filled[r : r + 1, :], COLS)
        stays[r] = jnp.where(live, jnp.where(lane != slot - 1, 2, 1), 0)
        cells = to_column(lax.rem(arrivals[r, 0], COLS), 16)
        slots = to_column(arrivals[r, 1], 16)
        hit = slots == iota((16, LANES), 1)
        number = jnp.sum(jnp.where(hit, iota((16, LANES), 0) + 1, 0), axis=0, keepdims=True) - 1
        cell = jnp.sum(jnp.where(hit, cells, 0), axis=0, keepdims=True)
        landing[8 * r : 8 * r + 1, :] = number
        landing[8 * r + 1 : 8 * r + 2, :] = jnp.where(number >= 0, cell, -1)
        wide = jnp.broadcast_to(slot - 1, (COLS, LANES))
        first_index, heading, target = hits[r]
        own_first = first_index == wide
        own_second = (heading == 0) & (target == wide)
        from_left = (heading == 2) & (target == roll_cells(wide, -1))
        if r == 1:
            _, above, aim = hits[0]
            straight = (above == 1) & (aim == wide)
            slant = (above == 3) & (aim == roll_cells(wide, -1))
            back = (above == 4) & (aim == roll_cells(wide, 1))
        info = jnp.where(lane == LIVE + 7, slot.astype(jnp.float32), which.astype(jnp.float32))
        for j in range(7):
            base = (r * 8 + j) * COLS
            f = on_first[base : base + COLS, :]
            s = on_second[base : base + COLS, :]
            total = jnp.where(own_first, f, 0.0) + jnp.where(own_second, s, 0.0)
            right = jnp.where(from_left, s, 0.0)
            if r == 1:
                u = on_second[j * COLS : (j + 1) * COLS, :]
                total = total + jnp.where(straight, u, 0.0)
                right = right + jnp.where(slant, u, 0.0)
                total = total + roll_cells(jnp.where(back, u, 0.0), -1)
            total = total + roll_cells(right, 1)
            info = jnp.where(lane == LIVE + j, jnp.sum(total, axis=1, keepdims=True), info)
        infos[r] = info

    turn = lax.rem(lax.axis_index("blade"), 2)
    for out, row in ((to_near, 1 - turn), (to_far, turn)):
        n = jnp.where(row == 1, counted[1], counted[0])
        lists = [pairs[k, row] for k in range(2)]
        for j in range(COMPS):
            value = packed(j, particles[j, row], lists, jnp.broadcast_to(n, (COLS, LANES)), infos[row])
            out[j * COLS : (j + 1) * COLS, :] = value


def edge_terms(
    got_near, got_far, sent_near, sent_far, infos, near_in, far_in, to_far, to_near, edges, edge_first, edge_second
):
    to_near[0:EDGE, :] = near_in[0:EDGE, :]
    to_far[0:EDGE, :] = far_in[0:EDGE, :]
    odd = lax.rem(lax.axis_index("span"), 2) == 1
    west = jnp.where(odd, got_near[...], got_far[...])
    east = jnp.where(odd, got_far[...], got_near[...])
    west_own = jnp.where(odd, sent_near[...], sent_far[...])
    east_own = jnp.where(odd, sent_far[...], sent_near[...])
    for k, side in enumerate((west, west_own, east_own, east)):
        for r in range(2):
            edges[pl.ds(4 * r + k, 12, stride=8), :] = side[r * 12 : r * 12 + 12]
    tile = [edges[j * 8 : j * 8 + 8, :] for j in range(COMPS)]
    first_index, second_index = unpacked(tile[:8])
    heading = second_index // LANES
    target = lax.rem(second_index, LANES)
    spot = iota((8, LANES), 0)
    lane = iota((8, LANES), 1)
    even = lax.rem(spot, 2) == 0
    listed = lane < lane_of(tile[8], 0).astype(jnp.int32)
    listed = listed & (
        ((heading == 2) & even)
        | ((heading == 3) & even & (spot < 4))
        | ((heading == 4) & ~even & (spot < 4))
    )
    first = [pick(t, first_index) for t in tile]
    second = []
    for t in tile:
        beside = pick(roll_cells(t, -1), target)
        below = pick(jnp.where(even, roll_cells(t, -5), roll_cells(t, -3)), target)
        second.append(jnp.where(heading == 2, beside, below))
    row_shift, col_shift = shifts(heading)
    f, s = pair_terms(first, second, row_shift, col_shift, listed)
    keep(edge_first, 0, f)
    keep(edge_second, 0, s)

    slots = [[lane_of(infos[r, c : c + 1, :], 7).astype(jnp.int32) for c in (0, COLS - 1)] for r in range(2)]

    def at_spots(*choices):
        value = jnp.zeros((8, LANES), jnp.int32)
        for k, slot in choices:
            value = jnp.where(spot == k, slot, value)
        return value - 1

    mine = first_index == at_spots((1, slots[0][0]), (2, slots[0][1]), (6, slots[1][1]))
    beside = (heading == 2) & (target == at_spots((0, slots[0][0]), (4, slots[1][0])))
    below = (heading != 2) & (target == at_spots((0, slots[1][0]), (3, slots[1][1])))
    sums = [jnp.zeros((8, LANES), jnp.float32)] * 3
    for j in range(7):
        for k, (hit, term) in enumerate(((mine, f[j]), (beside, s[j]), (below, s[j]))):
            total = jnp.sum(jnp.where(hit, term, 0.0), axis=1, keepdims=True)
            sums[k] = jnp.where(lane == LIVE + j, total, sums[k])
    fixes = (
        (sums[0][1:2] + sums[1][0:1], sums[0][2:3]),
        (sums[1][4:5] + sums[2][0:1], sums[0][6:7] + sums[2][3:4]),
    )
    turn = lax.rem(lax.axis_index("blade"), 2)
    for out, row in ((to_near, 1 - turn), (to_far, turn)):
        low = row == 1
        for k, c in enumerate((0, COLS - 1)):
            at = 9 * COLS + c
            out[at : at + 1, :] += jnp.where(low, fixes[1][k], fixes[0][k])
        out[EDGE : EDGE + 12, :] = jnp.where(low, east[12:24], east[0:12])
        out[EDGE + 12 : EDGE + 24, :] = jnp.where(low, west[12:24], west[0:12])


def own_sums(
    particles, pairs, count, on_first, on_second, edges, edge_first, edge_second,
    ext_in, sums, ext, first_low, lists_low, hot_low, by_source0, by_source1,
):
    ext[...] = ext_in[...]
    sizes = (40, 16)
    for ref, size in ((by_source0, 40), (by_source1, 16)):
        ref[0:size, :] = jnp.zeros((size, LANES), jnp.float32)
        ref[33 * size : 34 * size, :] = jnp.zeros((size, LANES), jnp.float32)
    blank = jnp.zeros((8, LANES), jnp.float32)
    for r, (ref, headings) in enumerate(((by_source0, (0, 1, 2, 3, 4)), (by_source1, (0, 2)))):

        def source(c, _, r=r, ref=ref, headings=headings):
            f = on_first[pl.ds(r * 8 * COLS + c, 8, stride=COLS), :]
            s = on_second[pl.ds(r * 8 * COLS + c, 8, stride=COLS), :]
            second_row = pairs[1, r, pl.ds(c, 1), :]
            heading = second_row // LANES
            left = jnp.concatenate(
                [jnp.concatenate([f if d == 0 else blank, jnp.where(heading == d, s, 0.0)], 1) for d in headings],
                0,
            )
            out = spread(left, pairs[0, r, pl.ds(c, 1), :], lax.rem(second_row, LANES))
            size = sizes[r]
            ref[pl.ds(pl.multiple_of((c + 1) * size, 8), size), :] = out
            return 0

        lax.fori_loop(0, COLS, source, 0, unroll=32)
    tile = [edges[j * 8 : j * 8 + 8, :] for j in range(COMPS)]
    first_index, second_index = unpacked(tile[:8])
    heading = second_index // LANES
    target = lax.rem(second_index, LANES)
    for k in (0, 1, 2, 3, 4, 6):
        f = edge_first[pl.ds(k, 8, stride=8), :]
        s = edge_second[pl.ds(k, 8, stride=8), :]
        aim = heading[k : k + 1]
        left = jnp.concatenate(
            [
                jnp.concatenate([f, blank], 1),
                jnp.concatenate([blank, jnp.where(aim == 2, s, 0.0)], 1),
                jnp.concatenate([blank, jnp.where(aim == 2, 0.0, s)], 1),
                jnp.zeros((8, 2 * LANES), jnp.float32),
            ],
            0,
        )
        out = spread(left, first_index[k : k + 1], target[k : k + 1])
        if k == 0:
            by_source0[16:24, :] = out[8:16]
            by_source0[24:32, :] = out[16:24]
        elif k == 1:
            by_source0[40:48, :] += out[0:8]
        elif k == 2:
            by_source0[32 * 40 : 32 * 40 + 8, :] += out[0:8]
        elif k == 3:
            by_source0[33 * 40 + 32 : 33 * 40 + 40, :] = out[16:24]
        elif k == 4:
            by_source1[8:16, :] = out[8:16]
        else:
            by_source1[32 * 16 : 32 * 16 + 8, :] += out[0:8]

    def column(ref, size, tile_at, shift, j):
        return ref[pl.ds((1 + shift) * size + tile_at * 8 + j, COLS, stride=size), :]

    for j in range(7):
        sums[0, j] = column(by_source0, 40, 0, 0, j) + column(by_source0, 40, 2, -1, j)
        total = column(by_source1, 16, 0, 0, j) + column(by_source1, 16, 1, -1, j)
        total = total + column(by_source0, 40, 1, 0, j) + column(by_source0, 40, 3, -1, j)
        sums[1, j] = total + column(by_source0, 40, 4, 1, j)

    for r in range(2):
        for j in range(COMPS):
            for k, at in ((3, 40), (0, 41), (1, 42), (0, 7)):
                ext[j, r, at : at + 1, :] = tile[j][4 * r + k : 4 * r + k + 1]
    rows = jnp.concatenate([pairs[0, 1], first_index[7:8], first_index[4:5], jnp.zeros((6, LANES), jnp.int32)], 0)
    seconds = jnp.concatenate([pairs[1, 1], second_index[7:8], second_index[4:5], jnp.zeros((6, LANES), jnp.int32)], 0)
    edge_count = lane_of(tile[8], 0).astype(jnp.int32)
    n = jnp.concatenate(
        [to_column(count[1:2, :], COLS), edge_count[7:8], edge_count[4:5], jnp.zeros((6, 1), jnp.int32)], 0
    )
    lists_low[0] = rows
    lists_low[1] = jnp.where(iota((SLAB, LANES), 1) < n, seconds // LANES, -1)
    lists_low[2] = lax.rem(seconds, LANES)
    for c in range(COLS):
        hot_low[c] = one_hot(pairs[0, 1, c : c + 1, :])
    for j in range(COMPS):
        first_low[j] = pick(ext[j, 1, BASE : BASE + SLAB, :], rows)


def surround(around, source):
    zeros = jnp.zeros((8, LANES), jnp.float32)
    for j in range(COMPS):
        main = source[j * COLS : (j + 1) * COLS, :]
        right = source[EDGE + j : EDGE + j + 1, :]
        left = source[EDGE + 12 + j : EDGE + 13 + j, :]
        around[j, 40:48, :] = zeros
        around[j, 8:40, :] = main
        around[j, 40:41, :] = right
        around[j, 41:42, :] = left
        around[j, 42:43, :] = main[0:1]
        around[j, 7:8, :] = left


def row_terms(first, others, heading, target):
    _, col_shift = shifts(heading)
    pieces = []
    for g in range(0, SLAB, 8):
        rows = slice(g, g + 8)
        aim = heading[rows]
        second = []
        for j in range(COMPS):
            value = None
            for d in (1, 3, 4):
                got = pick(others(j, BASE + col_steps[d] + g), target[rows])
                value = got if value is None else jnp.where(aim == d, got, value)
            second.append(value)
        listed = (aim == 1) | (aim == 3) | (aim == 4)
        pieces.append(pair_terms([first(j, rows) for j in range(COMPS)], second, 1.0, col_shift[rows], listed))
    return [[jnp.concatenate([piece[k][j] for piece in pieces], 0) for j in range(7)] for k in range(2)]


def finish(side, info, state, leaving, totals, ext, stays, landing, write):
    slot = lane_of(info, 7).astype(jnp.int32)
    which = lane_of(info, 8).astype(jnp.int32)
    leaves = slot > 0
    leaving = [t + lane_of(info, j) for j, t in enumerate(leaving)]
    at_slot = jnp.broadcast_to(jnp.maximum(slot - 1, 0), (COLS, LANES))
    moved = stepped([pick(v, at_slot) for v in state], leaving, leaves)
    moved[0] = moved[0] + (-1.0 if side == 0 else 1.0)
    match = (which == landing[8 * side : 8 * side + 1, :]) & leaves
    rows = stepped([ext[j, side, BASE : BASE + COLS, :] for j in range(COMPS)], totals, stays[side] > 0)
    lands = iota((COLS, LANES), 0) == landing[8 * side + 1 : 8 * side + 2, :]
    for j in range(COMPS):
        value = jnp.sum(jnp.where(match, moved[j], 0.0), axis=0, keepdims=True)
        write(side, j, jnp.where(lands, value, jnp.where(stays[side] == 1, 0.0, rows[j])))


def from_behind(source, sums, ext, stays, landing, write, around, terms, indices, by_source):
    surround(around, source)
    lane = iota((SLAB, LANES), 1)
    rows = [around[j, BASE : BASE + SLAB, :] for j in range(COMPS)]
    firsts, seconds = unpacked(rows[:8])
    heading = jnp.where(lane < lane_of(rows[8], 0).astype(jnp.int32), seconds // LANES, -1)
    target = lax.rem(seconds, LANES)
    f, s = row_terms(
        lambda j, at: pick(rows[j][at], firsts[at]), lambda j, at: ext[j, 0, at : at + 8, :], heading, target
    )
    keep(terms, 0, s)
    indices[0] = heading
    indices[1] = target
    for c in range(SOURCES):
        term = terms[pl.ds(c, 8, stride=SLAB), :]
        aim = indices[0, c : c + 1, :]
        left = jnp.concatenate([jnp.where(aim == d, term, 0.0) for d in (1, 3, 4)], 0)
        by_source[(c + 1) * 24 : (c + 2) * 24, :] = spread(left, indices[1, c : c + 1, :])
    by_source[0:24, :] = by_source[34 * 24 : 35 * 24, :]
    info = rows[9][:COLS]
    hit = firsts[:COLS] == lane_of(info, 7).astype(jnp.int32) - 1
    leaving = [jnp.sum(jnp.where(hit, f[j][:COLS], 0.0), axis=1, keepdims=True) for j in range(7)]
    totals = []
    for j in range(7):
        total = sums[0, j]
        for k, shift in ((0, 0), (1, -1), (2, 1)):
            total = total + by_source[pl.ds((1 + shift) * 24 + k * 8 + j, COLS, stride=24), :]
        totals.append(total)
    state = [v[:COLS] for v in rows]
    finish(0, info, state, leaving, totals, ext, stays, landing, write)


def from_ahead(source, sums, ext, first_low, lists_low, hot_low, stays, landing, write, around, terms, by_source):
    surround(around, source)
    heading, target = lists_low[1], lists_low[2]
    f, s = row_terms(
        lambda j, at: first_low[j, at, :], lambda j, at: around[j, at : at + 8, :], heading, target
    )
    keep(terms, 0, f)
    for c in range(COLS):
        by_source[c * 8 : c * 8 + 8, :] = gather_sums(terms[pl.ds(c, 8, stride=SLAB), :], hot_low[c])
    info = around[9, BASE : BASE + COLS, :]
    wide = jnp.broadcast_to(lane_of(info, 7).astype(jnp.int32) - 1, (COLS, LANES))
    wide = jnp.concatenate([wide, jnp.full((8, LANES), -1, jnp.int32)], 0)
    up = jnp.where(iota((SLAB, LANES), 0) == 33, wide[0:1], roll_cells(wide, -1))
    straight = (heading == 1) & (target == wide)
    slanting = (heading == 3) & (target == up)
    back = (heading == 4) & (target == roll_cells(wide, 1))
    first_cell = iota((COLS, LANES), 0) == 0
    leaving = []
    for j in range(7):
        slant = jnp.where(slanting, s[j], 0.0)
        slant = jnp.where(first_cell, slant[33:34], roll_cells(slant, 1)[:COLS])
        total = jnp.where(straight, s[j], 0.0)[:COLS] + slant
        total = total + roll_cells(jnp.where(back, s[j], 0.0), -1)[:COLS]
        leaving.append(jnp.sum(total, axis=1, keepdims=True))
    totals = [sums[1, j] + by_source[pl.ds(j, COLS, stride=8), :] for j in range(7)]
    state = [around[j, BASE : BASE + COLS, :] for j in range(COMPS)]
    finish(1, info, state, leaving, totals, ext, stays, landing, write)


def far_row(far, sums, ext, first_low, lists_low, hot_low, stays, landing, half, around, terms, indices, by_source):
    odd = lax.rem(lax.axis_index("blade"), 2) == 1

    def write(side, j, value):
        half[j] = value

    @pl.when(odd)
    def _():
        from_ahead(far, sums, ext, first_low, lists_low, hot_low, stays, landing, write, around, terms, by_source)

    @pl.when(jnp.logical_not(odd))
    def _():
        from_behind(far, sums, ext, stays, landing, write, around, terms, indices, by_source)


def near_row(near, half, sums, ext, first_low, lists_low, hot_low, stays, landing, out, around, terms, indices, by_source):
    odd = lax.rem(lax.axis_index("blade"), 2) == 1

    def write(side, j, value):
        out[j, side] = value
        out[j, 1 - side] = half[j]

    @pl.when(odd)
    def _():
        from_behind(near, sums, ext, stays, landing, write, around, terms, indices, by_source)

    @pl.when(jnp.logical_not(odd))
    def _():
        from_ahead(near, sums, ext, first_low, lists_low, hot_low, stays, landing, write, around, terms, by_source)


def swapped(block, axis, start):
    pairs = []
    for i in range(start, lax.axis_size(axis) - 1, 2):
        pairs += [(i, i + 1), (i + 1, i)]
    return lax.ppermute(block, axis, pairs)


vmem = pl.BlockSpec(memory_space=pltpu.VMEM)
smem = pl.BlockSpec(memory_space=pltpu.SMEM)
hbm = pl.BlockSpec(memory_space=pltpu.HBM)
params = pltpu.CompilerParams(vmem_limit_bytes=24 * 1024 * 1024)


def shape(*dims, dtype=jnp.float32):
    return jax.ShapeDtypeStruct(dims, dtype)


def buffer(*dims, dtype=jnp.float32):
    return pltpu.VMEM(dims, dtype)


def body(particles, filled, contact_pairs, contact_count, movers_out, movers_in, move_count):
    ints = jnp.int32
    far, near = pl.pallas_call(
        pack_columns,
        in_specs=[hbm] * 3,
        out_specs=[vmem] * 2,
        out_shape=[shape(24, LANES)] * 2,
        scratch_shapes=[
            buffer(COMPS, 2, 1, LANES),
            buffer(COMPS, 2, 1, LANES),
            buffer(2, 2, 1, LANES, dtype=ints),
            buffer(2, 2, 1, LANES, dtype=ints),
            buffer(2, COLS, dtype=ints),
            pltpu.SemaphoreType.DMA((5,)),
        ],
        compiler_params=params,
        name="pack_columns",
    )(*(pltpu.with_memory_space_constraint(x, pltpu.HBM) for x in (particles, contact_pairs, contact_count)))
    got_far = swapped(far, "span", 1)
    got_near = swapped(near, "span", 0)
    on_first, on_second, to_near, to_far, ext, infos, stays, landing = pl.pallas_call(
        inner_terms,
        in_specs=[vmem] * 6 + [smem],
        out_specs=[vmem] * 8,
        out_shape=[
            shape(17 * COLS, LANES),
            shape(17 * COLS, LANES),
            shape(PAYLOAD, LANES),
            shape(PAYLOAD, LANES),
            shape(COMPS, 2, EXT, LANES),
            shape(2, COLS, LANES),
            shape(2, COLS, LANES, dtype=ints),
            shape(16, LANES, dtype=ints),
        ],
        compiler_params=params,
        name="inner_terms",
    )(particles, contact_pairs, contact_count, filled, movers_out, movers_in, move_count)
    to_far, to_near, edges, edge_first, edge_second = pl.pallas_call(
        edge_terms,
        in_specs=[vmem] * 7,
        out_specs=[vmem] * 5,
        out_shape=[
            shape(PAYLOAD, LANES),
            shape(PAYLOAD, LANES),
            shape(104, LANES),
            shape(72, LANES),
            shape(72, LANES),
        ],
        compiler_params=params,
        name="edge_terms",
    )(got_near, got_far, near, far, infos, to_near, to_far)
    row_far = swapped(to_far, "blade", 1)
    row_near = swapped(to_near, "blade", 0)
    sums, ext, first_low, lists_low, hot_low = pl.pallas_call(
        own_sums,
        in_specs=[vmem] * 9,
        out_specs=[vmem] * 5,
        out_shape=[
            shape(2, 7, COLS, LANES),
            shape(COMPS, 2, EXT, LANES),
            shape(COMPS, SLAB, LANES),
            shape(3, SLAB, LANES, dtype=ints),
            shape(COLS, LANES, LANES, dtype=jnp.bfloat16),
        ],
        scratch_shapes=[buffer(35 * 40, LANES), buffer(34 * 16, LANES)],
        compiler_params=params,
        name="own_sums",
    )(particles, contact_pairs, contact_count, on_first, on_second, edges, edge_first, edge_second, ext)
    own = (sums, ext, first_low, lists_low, hot_low, stays, landing)
    scratch = [
        buffer(COMPS, EXT, LANES),
        buffer(9 * SLAB, LANES),
        buffer(2, SLAB, LANES, dtype=ints),
        buffer(35 * 24, LANES),
    ]
    half = pl.pallas_call(
        far_row,
        in_specs=[vmem] * 8,
        out_specs=vmem,
        out_shape=shape(COMPS, COLS, LANES),
        scratch_shapes=scratch,
        compiler_params=params,
        name="far_row",
    )(row_far, *own)
    return pl.pallas_call(
        near_row,
        in_specs=[vmem] * 9,
        out_specs=vmem,
        out_shape=shape(COMPS, 2, COLS, LANES),
        scratch_shapes=scratch,
        compiler_params=params,
        name="near_row",
    )(row_near, half, *own)


def solution(mesh):
    return jax.shard_map(
        body,
        mesh=mesh,
        in_specs=(
            P(None, "blade", "span", None),
            P("blade", "span"),
            P(None, "blade", "span", None),
            P("blade", "span"),
            P(None, None, "blade", "span"),
            P(None, None, "blade", "span"),
            P(None, "blade", "span"),
        ),
        out_specs=P(None, "blade", "span", None),
        check_vma=False,
    )
```
